512 devices in a mesh: axial: 16 (over y, x), cross: 32 (over z, core).
Axes of the slice: x: 4, y: 4, z: 16, core: 2. Of those that a mesh axis runs over, the one named last changes fastest.
Arguments:
- force: float32 [16, 32, 8, 3, 128], P('axial', 'cross'), may hold values from -6 to 6
- self_drag: float32 [16, 32, 8, 128], P('axial', 'cross'), may hold values from 0.5 to 4
- tiles: bfloat16 [16, 32, 8, 8, 128, 128], P('axial', 'cross'), may hold values from -0.1875 to 0.1875
- tile_ids: int32 [16, 32, 8, 8], P('axial', 'cross'), may hold values from 8 to 63, as said below
- mig_rows: int32 [16, 32, 2, 64], P('axial', 'cross'), may hold values from 0 to 1023, as said below
- mig_count: int32 [16, 32, 2], P('axial', 'cross'), may hold values from 0 to 64, as said below
Outputs:
- velocity: float32 [16, 32, 8, 3, 128], P('axial', 'cross')
- residual: float32 [16, 32, 8, 3, 128], P('axial', 'cross')
- arrivals: float32 [16, 32, 3, 128], P('axial', 'cross')
The draws below stay inside these ranges and needn't reach their ends.
Inputs may be any that keep to these rules, and one draw needn't show every extreme that they name: `tile_ids`: each entry is p * 8 + q with p one of 1, 3, 4, 5, 7 and q below 8; the first five tiles of every block name the five values of p. `mig_rows`: the 128 entries of one device are distinct beads. `mig_count`: the lowest slab sends nothing to the lower side and the highest nothing to the upper side; in every axial group one slab sends 64 beads to both sides.
All inputs are finite; a program needn't handle non-finite values.
Results may differ from the reference program's by a relative error of at most 0.024.
Values may be sent and summed in bfloat16 or wider, within the bound.
No kernel may reach another device: no remote copies, remote signals or barrier semaphores. Data moves between devices by JAX's collectives and lax.ppermute only.
A program may use at most 64 MiB of HBM per device.

```python
import math
import jax
import jax.numpy as jnp
from jax import lax

BLOCK = 128
TILES = 8
BLK_DEV = 8
SLOT = 64
ITERS = 3
AXIAL_GROUPS = 16
SLABS = 32


def draw_tile_ids(key, part):
    first, second, third = jax.random.split(key, 3)
    shape = (AXIAL_GROUPS, SLABS, BLK_DEV, TILES)
    offset = jax.random.randint(first, (AXIAL_GROUPS, SLABS, BLK_DEV, 1), 0, 5)
    spare = jax.random.randint(second, shape, 0, 5)
    column = lax.broadcasted_iota(jnp.int32, shape, 3)
    region = jnp.where(column < 5, (offset + column) % 5, spare)
    table = jnp.array([4, 1, 7, 3, 5], dtype=jnp.int32)
    place = jnp.take(table, region)
    member = jax.random.randint(third, shape, 0, BLK_DEV)
    return (place * BLK_DEV + member).astype(jnp.int32)


def draw_mig_rows(key, part):
    keys = jax.random.split(jax.random.fold_in(key, 11), AXIAL_GROUPS * SLABS)

    def one_device(device_key):
        return jax.random.permutation(device_key, BLK_DEV * BLOCK)[:2 * SLOT]
    chosen = jax.vmap(one_device)(keys)
    return chosen.reshape(AXIAL_GROUPS, SLABS, 2, SLOT).astype(jnp.int32)


def draw_mig_count(key, part):
    first, second = jax.random.split(jax.random.fold_in(key, 23), 2)
    shape = (AXIAL_GROUPS, SLABS, 2)
    counts = jax.random.randint(first, shape, (SLOT + 2) // 3, SLOT + 1)
    target = jax.random.randint(second, (AXIAL_GROUPS, 1, 1), 1, SLABS - 1)
    slab = lax.broadcasted_iota(jnp.int32, shape, 1)
    side = lax.broadcasted_iota(jnp.int32, shape, 2)
    counts = jnp.where(slab == target, SLOT, counts)
    edge = jnp.logical_or(jnp.logical_and(side == 0, slab == 0), jnp.logical_and(side == 1, slab == SLABS - 1))
    return jnp.where(edge, 0, counts).astype(jnp.int32)


def level_of(rng, shape, cuts, least, largest):
    def one(position, blocks):
        heights = jax.random.uniform(jax.random.fold_in(jax.random.fold_in(rng, 6), position), (blocks,), jnp.float32, least / len(cuts), largest / len(cuts))
        return jnp.repeat(jnp.exp(heights), shape[position] // blocks).reshape((-1,) + (1,) * (len(shape) - position - 1))

    gain = one(*cuts[0])
    for cut in cuts[1:]:
        gain = gain * one(*cut)
    return gain


def bell_draw(rng, shape, deviation, reach, cuts=(), kind=jnp.bfloat16):
    level = level_of(rng, shape, cuts, -0.22, 0.18) if cuts else 1.0
    values = jax.random.normal(rng, shape, jnp.float32) * deviation * level
    return jnp.minimum(jnp.maximum(values, -reach), reach).astype(kind)


def setup_inputs(seed: int = 0) -> dict:
    key_of = jax.random.split(jax.random.key(seed), 7)
    return {
        "force": bell_draw(key_of[0], (AXIAL_GROUPS, SLABS, BLK_DEV, 3, BLOCK), 1.0, 6.0, ((0, 16), (1, 32)), jnp.float32),
        "self_drag": jnp.clip(jnp.exp(math.log(4.0) - 2.0794415 * jax.random.uniform(key_of[1], (AXIAL_GROUPS, SLABS, BLK_DEV, BLOCK), jnp.float32) ** level_of(key_of[1], (AXIAL_GROUPS, SLABS, BLK_DEV, BLOCK), ((0, 16), (1, 32)), -0.2, 0.2)), 0.5, 4.0),
        "tiles": bell_draw(key_of[2], (AXIAL_GROUPS, SLABS, BLK_DEV, TILES, BLOCK, BLOCK), (TILES * BLOCK) ** -0.5, 0.1875, ((0, 16), (1, 32))),
        "tile_ids": draw_tile_ids(jax.random.fold_in(key_of[6], 71), 0),
        "mig_rows": draw_mig_rows(jax.random.fold_in(key_of[6], 71), 0),
        "mig_count": draw_mig_count(jax.random.fold_in(key_of[6], 71), 0),
    }


def extended_list(field):
    blanks = jnp.zeros_like(field)
    below_axial = jnp.roll(field, 1, axis=0)
    above_axial = jnp.roll(field, -1, axis=0)
    below_cross = jnp.concatenate([blanks[:, :1], field[:, :-1]], axis=1)
    above_cross = jnp.concatenate([field[:, 1:], blanks[:, :1]], axis=1)
    stacked = jnp.stack([blanks, below_axial, blanks, below_cross, field, above_cross, blanks, above_axial, blanks], axis=2)
    return stacked.reshape(AXIAL_GROUPS * SLABS, 9 * BLK_DEV, 3, BLOCK)


def device_product(operands):
    extended, tile_block, id_block = operands
    picked = extended[id_block].astype(jnp.float32)
    tile_wide = tile_block.astype(jnp.float32)
    coupled = jnp.einsum("bkij,bkcj->bci", tile_wide, picked).astype(jnp.bfloat16)
    spread = jnp.einsum("bkij,bci->bkcj", tile_wide, coupled.astype(jnp.float32))
    return jax.ops.segment_sum(spread.reshape(-1, 3, BLOCK), id_block.reshape(-1), num_segments=9 * BLK_DEV)


def apply_operator(direction, self_drag, tiles, tile_ids):
    lowered = direction.astype(jnp.bfloat16)
    extended = extended_list(lowered)
    flat_tiles = tiles.reshape(AXIAL_GROUPS * SLABS, BLK_DEV, TILES, BLOCK, BLOCK)
    flat_ids = tile_ids.reshape(AXIAL_GROUPS * SLABS, BLK_DEV, TILES)
    returned = lax.map(device_product, (extended, flat_tiles, flat_ids))
    returned = returned.reshape(AXIAL_GROUPS, SLABS, 9, BLK_DEV, 3, BLOCK)
    zeros_slab = jnp.zeros_like(returned[:, :1, 0])
    total = returned[:, :, 4]
    total = total + jnp.roll(returned[:, :, 1], -1, axis=0)
    total = total + jnp.roll(returned[:, :, 7], 1, axis=0)
    total = total + jnp.concatenate([returned[:, 1:, 3], zeros_slab], axis=1)
    total = total + jnp.concatenate([zeros_slab, returned[:, :-1, 5]], axis=1)
    return self_drag[:, :, :, None, :] * direction + total


def pick_rows(flat, rows):
    return flat[:, rows.reshape(-1)]


def reference(force, self_drag, tiles, tile_ids, mig_rows, mig_count):
    velocity = jnp.zeros_like(force)
    residual = force
    direction = force
    norm_now = jnp.sum(residual * residual)
    for sweep in range(ITERS):
        image = apply_operator(direction, self_drag, tiles, tile_ids)
        alpha = norm_now / jnp.sum(direction * image)
        velocity = velocity + alpha * direction
        residual = residual - alpha * image
        norm_next = jnp.sum(residual * residual)
        direction = residual + (norm_next / norm_now) * direction
        norm_now = norm_next
    flat = jnp.swapaxes(velocity, 2, 3).reshape(AXIAL_GROUPS, SLABS, 3, BLK_DEV * BLOCK)
    picked = jax.vmap(jax.vmap(pick_rows))(flat, mig_rows)
    picked = picked.reshape(AXIAL_GROUPS, SLABS, 3, 2, SLOT)
    live = jnp.arange(SLOT, dtype=jnp.int32)[None, None, None, None, :] < mig_count[:, :, None, :, None]
    sent = jnp.where(live, picked, jnp.zeros_like(picked))
    blank = jnp.zeros_like(sent[:, :1, :, 0])
    from_lower = jnp.concatenate([blank, sent[:, :-1, :, 1]], axis=1)
    from_upper = jnp.concatenate([sent[:, 1:, :, 0], blank], axis=1)
    arrivals = jnp.concatenate([from_lower, from_upper], axis=3)
    return velocity, residual, arrivals
```

```python
import jax
import jax.numpy as jnp
from jax import lax
from jax.experimental import pallas as pl
from jax.experimental.pallas import tpu as pltpu
from jax.sharding import PartitionSpec as P

ITERS = 3
PLACES = (1, 3, 4, 5, 7)
SUB = 8
LOW = 4


def ring(count, by):
    return [(i, (i + by) % count) for i in range(count)]


def ring_shift(shard, axis, by):
    return lax.ppermute(shard, axis, ring(lax.axis_size(axis), by))


def high_low(x):
    high = x.astype(jnp.bfloat16).astype(jnp.float32)
    return high, x - high


def operator_kernel(
    ids, own, from_axial_dn, from_cross_dn, from_cross_up, from_axial_up, tiles, drag,
    to_axial_dn, to_cross_dn, to_cross_up, to_axial_up, kept, moments, ext, acc,
):
    blocks, count = ids.shape
    width = tiles.shape[-1]
    slab = lax.axis_index("cross")
    has_dn = jnp.where(slab > 0, 1.0, 0.0).astype(jnp.float32)
    has_up = jnp.where(slab < lax.axis_size("cross") - 1, 1.0, 0.0).astype(jnp.float32)
    sources = (from_axial_dn, from_cross_dn, own, from_cross_up, from_axial_up)
    blank = jnp.zeros((blocks, width), jnp.float32)
    for place, source in zip(PLACES, sources):
        base = place * blocks * SUB
        for comp in range(3):
            x = source[comp]
            if place == 3:
                x = x * has_dn
            if place == 5:
                x = x * has_up
            high, low = high_low(x)
            ext[pl.ds(base + comp, blocks, stride=SUB), :] = high
            ext[pl.ds(base + LOW + comp, blocks, stride=SUB), :] = low
        ext[pl.ds(base + 3, blocks, stride=SUB), :] = blank
        ext[pl.ds(base + LOW + 3, blocks, stride=SUB), :] = blank
    acc[...] = jnp.zeros_like(acc)
    rows = lax.broadcasted_iota(jnp.int32, (SUB, width), 0)
    squares = jnp.zeros((SUB, width), jnp.float32)
    for b in range(blocks):
        starts = [pl.multiple_of(ids[b, k] * SUB, SUB) for k in range(count)]
        coupled = jnp.zeros((SUB, width), jnp.float32)
        for k in range(0, count, 2):
            picked = jnp.concatenate(
                [ext[pl.ds(starts[k], SUB), :], ext[pl.ds(starts[k + 1], SUB), :]], axis=1
            ).astype(jnp.bfloat16)
            pair = jnp.concatenate([tiles[b, k], tiles[b, k + 1]], axis=1)
            coupled += lax.dot_general(
                picked, pair, (((1,), (1,)), ((), ())), preferred_element_type=jnp.float32
            )
        coupled = coupled + pltpu.roll(coupled, LOW, 0)
        squares += jnp.where(rows < LOW, coupled * coupled, 0.0)
        high, low = high_low(coupled)
        parts = jnp.where(rows < LOW, high, low).astype(jnp.bfloat16)
        for k in range(count):
            acc[pl.ds(starts[k], SUB), :] += jnp.dot(
                parts, tiles[b, k], preferred_element_type=jnp.float32
            )
    targets = (to_axial_dn, to_cross_dn, None, to_cross_up, to_axial_up)
    even = jnp.zeros((blocks, width), jnp.float32)
    odd = squares
    for place, target in zip(PLACES, targets):
        base = place * blocks * SUB
        for comp in range(3):
            total = (
                acc[pl.ds(base + comp, blocks, stride=SUB), :]
                + acc[pl.ds(base + LOW + comp, blocks, stride=SUB), :]
            )
            if target is None:
                x = own[comp]
                dragged = drag[...] * x
                even += x * x
                odd += dragged * x
                kept[comp] = dragged + total
            else:
                target[comp] = total
    moments[0] = even
    moments[1] = odd


def operator_call(ids, sources, tiles, drag):
    blocks, width = drag.shape
    vmem = pl.BlockSpec(memory_space=pltpu.VMEM)
    field = jax.ShapeDtypeStruct((3, blocks, width), jnp.float32)
    return pl.pallas_call(
        operator_kernel,
        in_specs=[pl.BlockSpec(memory_space=pltpu.SMEM)] + [vmem] * 7,
        out_specs=[vmem] * 6,
        out_shape=[field] * 5 + [jax.ShapeDtypeStruct((2, blocks, width), jnp.float32)],
        scratch_shapes=[
            pltpu.VMEM((8 * blocks * SUB, width), jnp.float32),
            pltpu.VMEM((8 * blocks * SUB, width), jnp.float32),
        ],
        compiler_params=pltpu.CompilerParams(vmem_limit_bytes=24 << 20),
    )(ids, *sources, tiles, drag)


def shifted_poly(poly):
    return [None] + list(poly)


def combine(left, scale, right):
    out = []
    for i in range(max(len(left), len(right))):
        a = left[i] if i < len(left) else None
        b = right[i] if i < len(right) else None
        b = None if b is None else scale * b
        out.append(b if a is None else a if b is None else a + b)
    return out


def inner(left, right, shift, moment):
    total = None
    for i, a in enumerate(left):
        for j, b in enumerate(right):
            term = a * b * moment[i + j + shift]
            total = term if total is None else total + term
    return total


def cg_coefficients(moment):
    one = jnp.ones_like(moment[0])
    velocity, residual, direction = [], [one], [one]
    norm_now = moment[0]
    for sweep in range(ITERS):
        alpha = norm_now / inner(direction, direction, 1, moment)
        velocity = combine(velocity, alpha, direction)
        residual = combine(residual, -alpha, shifted_poly(direction))
        if sweep < ITERS - 1:
            norm_next = inner(residual, residual, 0, moment)
            direction = combine(residual, norm_next / norm_now, direction)
            norm_now = norm_next
    return velocity, residual


def mixed(coefs, fields):
    total = coefs[0] * fields[0]
    for c, f in zip(coefs[1:], fields[1:]):
        total = total + c * f
    return total


def picked_beads(fields, coefs, wanted, live):
    blocks, width = fields[0][0].shape
    index = jnp.where(live, wanted.astype(jnp.int32), -1)
    block = lax.shift_right_arithmetic(index, 7)
    place = jnp.bitwise_and(index, width - 1)
    parts = []
    for comp in range(3):
        x = mixed(coefs, [f[comp] for f in fields])
        high, rest = high_low(x)
        middle, low = high_low(rest)
        parts += [high, middle, low]
    stacked = jnp.concatenate(parts + [jnp.zeros_like(parts[0])], axis=0).astype(jnp.bfloat16)
    lanes = lax.broadcasted_iota(jnp.int32, (width, width), 0)
    chosen = jnp.where(lanes == place, 1.0, 0.0).astype(jnp.bfloat16)
    found = jnp.dot(stacked, chosen, preferred_element_type=jnp.float32)
    keep = lax.broadcasted_iota(jnp.int32, (blocks, width), 0) == block
    out = []
    for comp in range(3):
        at = 3 * comp * blocks
        x = (
            found[at : at + blocks]
            + found[at + blocks : at + 2 * blocks]
            + found[at + 2 * blocks : at + 3 * blocks]
        )
        out.append(jnp.sum(jnp.where(keep, x, 0.0), axis=0, keepdims=True))
    return out


def finish_kernel(sums, k0, k1, k2, k3, d0, d1, d2, u0, u1, u2, velocity, residual, arrivals):
    blocks, width = k0.shape[1:]
    slab = lax.axis_index("cross")
    total = jnp.sum(sums[...], axis=0)
    moment = [
        jnp.broadcast_to(jnp.sum(total[i : i + 1], axis=1, keepdims=True), (blocks, width))
        for i in range(2 * ITERS)
    ]
    vel, res = cg_coefficients(moment)
    own = (k0, k1, k2, k3)
    for comp in range(3):
        velocity[comp] = mixed(vel, [k[comp] for k in own[:ITERS]])
        residual[comp] = mixed(res, [k[comp] for k in own])
    lower = picked_beads((d0, d1, d2), vel, d0[3, 1:2, :], slab > 0)
    upper = picked_beads(
        (u0, u1, u2), vel, u0[3, 0:1, :], slab < lax.axis_size("cross") - 1
    )
    for comp in range(3):
        arrivals[comp : comp + 1, :] = lower[comp] + upper[comp]


def finish_call(sums, own, below, above):
    blocks, width = own[1].shape[1:]
    vmem = pl.BlockSpec(memory_space=pltpu.VMEM)
    field = jax.ShapeDtypeStruct((3, blocks, width), jnp.float32)
    return pl.pallas_call(
        finish_kernel,
        in_specs=[vmem] * 11,
        out_specs=[vmem] * 3,
        out_shape=[field, field, jax.ShapeDtypeStruct((3, width), jnp.float32)],
    )(sums, *own, *below, *above)


def leaving_rows(mig_rows, mig_count, blocks, width):
    capacity = mig_rows.shape[-1]
    live = lax.broadcasted_iota(jnp.int32, (2, capacity), 1) < mig_count[0, 0][:, None]
    rows = jnp.where(live, mig_rows[0, 0], -1).astype(jnp.float32)
    none = jnp.full((1, width - capacity), -1.0, jnp.float32)
    to_lower = jnp.concatenate([none, rows[0:1]], axis=1)
    to_upper = jnp.concatenate([rows[1:2], none], axis=1)
    rest = jnp.zeros((blocks - 2, width), jnp.float32)
    return jnp.concatenate([to_lower, to_upper, rest], axis=0)[None]


def spread_sum(part, axis):
    count = lax.axis_size(axis)
    copies = jnp.broadcast_to(part[None], (count,) + part.shape)
    return lax.all_to_all(copies, axis, 0, 0)


def on_device(force, self_drag, tiles, tile_ids, mig_rows, mig_count):
    field = jnp.swapaxes(force[0, 0], 0, 1)
    drag = self_drag[0, 0]
    blocks, width = drag.shape
    ids = tile_ids[0, 0]
    slab = lax.axis_index("cross")
    last = lax.axis_size("cross") - 1
    now = jnp.concatenate([field, leaving_rows(mig_rows, mig_count, blocks, width)], axis=0)
    own, below, above, moments = [], [], [], []
    for sweep in range(ITERS):
        cross_dn = ring_shift(now, "cross", 1)
        cross_up = ring_shift(now, "cross", -1)
        axial_dn = ring_shift(now[:3], "axial", 1)
        axial_up = ring_shift(now[:3], "axial", -1)
        own.append(now)
        below.append(cross_dn)
        above.append(cross_up)
        r1, r3, r5, r7, kept, pair = operator_call(
            ids, (now, axial_dn, cross_dn, cross_up, axial_up), tiles[0, 0], drag
        )
        moments.append(jnp.sum(pair, axis=1))
        from_lower_cross = ring_shift(r5, "cross", 1)
        from_upper_cross = ring_shift(r3, "cross", -1)
        from_lower_axial = ring_shift(r7, "axial", 1)
        from_upper_axial = ring_shift(r1, "axial", -1)
        now = kept + from_lower_axial + from_upper_axial
        now = now + jnp.where(slab > 0, from_lower_cross, 0.0)
        now = now + jnp.where(slab < last, from_upper_cross, 0.0)
    own.append(now)
    part = jnp.concatenate(moments + [jnp.zeros((2, width), jnp.float32)], axis=0)
    part = jnp.sum(spread_sum(part, "axial"), axis=0)
    sums = spread_sum(part, "cross")
    velocity, residual, arrivals = finish_call(sums, own, below, above)
    return (
        jnp.swapaxes(velocity, 0, 1)[None, None],
        jnp.swapaxes(residual, 0, 1)[None, None],
        arrivals[None, None],
    )


def solution(mesh):
    placed = (
        P("axial", "cross", None, None, None),
        P("axial", "cross", None, None),
        P("axial", "cross", None, None, None, None),
        P("axial", "cross", None, None),
        P("axial", "cross", None, None),
        P("axial", "cross", None),
    )
    return jax.shard_map(
        on_device,
        mesh=mesh,
        in_specs=placed,
        out_specs=(
            P("axial", "cross", None, None, None),
            P("axial", "cross", None, None, None),
            P("axial", "cross", None, None),
        ),
        check_vma=False,
    )
```

```python
import functools

import jax
import jax.numpy as jnp
from jax import lax
from jax.experimental import pallas as pl
from jax.experimental.pallas import tpu as pltpu
from jax.sharding import PartitionSpec as P

ITERS = 3
PLACES = (1, 3, 4, 5, 7)
SUB = 8
LOW = 4


def ring(count, by):
    return [(i, (i + by) % count) for i in range(count)]


def ring_shift(shard, axis, by):
    return lax.ppermute(shard, axis, ring(lax.axis_size(axis), by))


def high_low(x):
    high = x.astype(jnp.bfloat16).astype(jnp.float32)
    return high, x - high


def operator_kernel(
    sweep, ids, own, from_axial_dn, from_cross_dn, from_cross_up, from_axial_up, tiles, drag, carried,
    to_axial_dn, to_cross_dn, to_cross_up, to_axial_up, kept, moments, ext, acc,
):
    blocks, count = ids.shape
    width = tiles.shape[-1]
    slab = lax.axis_index("cross")
    has_dn = jnp.where(slab > 0, 1.0, 0.0).astype(jnp.float32)
    has_up = jnp.where(slab < lax.axis_size("cross") - 1, 1.0, 0.0).astype(jnp.float32)
    sources = (from_axial_dn, from_cross_dn, own, from_cross_up, from_axial_up)
    blank = jnp.zeros((blocks, width), jnp.float32)
    for place, source in zip(PLACES, sources):
        base = place * blocks * SUB
        for comp in range(3):
            x = source[comp]
            if place == 3:
                x = x * has_dn
            if place == 5:
                x = x * has_up
            high, low = high_low(x)
            ext[pl.ds(base + comp, blocks, stride=SUB), :] = high
            ext[pl.ds(base + LOW + comp, blocks, stride=SUB), :] = low
        ext[pl.ds(base + 3, blocks, stride=SUB), :] = blank
        ext[pl.ds(base + LOW + 3, blocks, stride=SUB), :] = blank
    acc[...] = jnp.zeros_like(acc)
    rows = lax.broadcasted_iota(jnp.int32, (SUB, width), 0)
    squares = jnp.zeros((SUB, width), jnp.float32)
    for b in range(blocks):
        starts = [pl.multiple_of(ids[b, k] * SUB, SUB) for k in range(count)]
        coupled = jnp.zeros((SUB, width), jnp.float32)
        for k in range(0, count, 2):
            picked = jnp.concatenate(
                [ext[pl.ds(starts[k], SUB), :], ext[pl.ds(starts[k + 1], SUB), :]], axis=1
            ).astype(jnp.bfloat16)
            pair = jnp.concatenate([tiles[b, k], tiles[b, k + 1]], axis=1)
            coupled += lax.dot_general(
                picked, pair, (((1,), (1,)), ((), ())), preferred_element_type=jnp.float32
            )
        coupled = coupled + pltpu.roll(coupled, LOW, 0)
        squares += jnp.where(rows < LOW, coupled * coupled, 0.0)
        high, low = high_low(coupled)
        parts = jnp.where(rows < LOW, high, low).astype(jnp.bfloat16)
        for k in range(count):
            acc[pl.ds(starts[k], SUB), :] += jnp.dot(
                parts, tiles[b, k], preferred_element_type=jnp.float32
            )
    targets = (to_axial_dn, to_cross_dn, None, to_cross_up, to_axial_up)
    even = jnp.zeros((blocks, width), jnp.float32)
    odd = squares
    for place, target in zip(PLACES, targets):
        base = place * blocks * SUB
        for comp in range(3):
            total = (
                acc[pl.ds(base + comp, blocks, stride=SUB), :]
                + acc[pl.ds(base + LOW + comp, blocks, stride=SUB), :]
            )
            if target is None:
                x = own[comp]
                dragged = drag[...] * x
                even += x * x
                odd += dragged * x
                kept[comp] = dragged + total
            else:
                target[comp] = total
    even = jnp.sum(even, axis=0, keepdims=True)
    odd = jnp.sum(odd, axis=0, keepdims=True)
    if sweep == 0:
        moments[...] = jnp.where(rows == 0, even, jnp.where(rows == 1, odd, 0.0))
        to_cross_dn[3] = carried[...]
        to_cross_up[3] = carried[...]
    else:
        moments[...] = jnp.where(
            rows == 2 * sweep, even, jnp.where(rows == 2 * sweep + 1, odd, carried[...])
        )


def operator_call(sweep, ids, sources, tiles, drag, carried):
    blocks, width = drag.shape
    vmem = pl.BlockSpec(memory_space=pltpu.VMEM)
    field = jax.ShapeDtypeStruct((3, blocks, width), jnp.float32)
    across = jax.ShapeDtypeStruct((4 if sweep == 0 else 3, blocks, width), jnp.float32)
    plane = jax.ShapeDtypeStruct((SUB, width), jnp.float32)
    return pl.pallas_call(
        functools.partial(operator_kernel, sweep),
        in_specs=[pl.BlockSpec(memory_space=pltpu.SMEM)] + [vmem] * 8,
        out_specs=[vmem] * 6,
        out_shape=[field, across, across, field, field, plane],
        scratch_shapes=[
            pltpu.VMEM((8 * blocks * SUB, width), jnp.float32),
            pltpu.VMEM((8 * blocks * SUB, width), jnp.float32),
        ],
        compiler_params=pltpu.CompilerParams(vmem_limit_bytes=4 << 20),
    )(ids, *sources, tiles, drag, carried)


def shifted_poly(poly):
    return [None] + list(poly)


def combine(left, scale, right):
    out = []
    for i in range(max(len(left), len(right))):
        a = left[i] if i < len(left) else None
        b = right[i] if i < len(right) else None
        b = None if b is None else scale * b
        out.append(b if a is None else a if b is None else a + b)
    return out


def inner(left, right, shift, moment):
    total = None
    for i, a in enumerate(left):
        for j, b in enumerate(right):
            term = a * b * moment[i + j + shift]
            total = term if total is None else total + term
    return total


def cg_coefficients(moment):
    one = jnp.ones_like(moment[0])
    velocity, residual, direction = [], [one], [one]
    norm_now = moment[0]
    for sweep in range(ITERS):
        alpha = norm_now / inner(direction, direction, 1, moment)
        velocity = combine(velocity, alpha, direction)
        residual = combine(residual, -alpha, shifted_poly(direction))
        if sweep < ITERS - 1:
            norm_next = inner(residual, residual, 0, moment)
            direction = combine(residual, norm_next / norm_now, direction)
            norm_now = norm_next
    return velocity, residual


def mixed(coefs, fields):
    total = coefs[0] * fields[0]
    for c, f in zip(coefs[1:], fields[1:]):
        total = total + c * f
    return total


def picked_beads(fields, coefs, wanted, live):
    blocks, width = fields[0][0].shape
    index = jnp.where(live, wanted.astype(jnp.int32), -1)
    block = lax.shift_right_arithmetic(index, 7)
    place = jnp.bitwise_and(index, width - 1)
    parts = []
    for comp in range(3):
        x = mixed(coefs, [f[comp] for f in fields])
        high, rest = high_low(x)
        middle, low = high_low(rest)
        parts += [high, middle, low]
    stacked = jnp.concatenate(parts + [jnp.zeros_like(parts[0])], axis=0).astype(jnp.bfloat16)
    lanes = lax.broadcasted_iota(jnp.int32, (width, width), 0)
    chosen = jnp.where(lanes == place, 1.0, 0.0).astype(jnp.bfloat16)
    found = jnp.dot(stacked, chosen, preferred_element_type=jnp.float32)
    keep = lax.broadcasted_iota(jnp.int32, (blocks, width), 0) == block
    out = []
    for comp in range(3):
        at = 3 * comp * blocks
        x = (
            found[at : at + blocks]
            + found[at + blocks : at + 2 * blocks]
            + found[at + 2 * blocks : at + 3 * blocks]
        )
        out.append(jnp.sum(jnp.where(keep, x, 0.0), axis=0, keepdims=True))
    return out


def finish_kernel(
    sums, k0, k1, k2, k3, d0, d1, d2, u0, u1, u2, dn_plane, up_plane, velocity, residual, arrivals
):
    blocks, width = k0.shape[1:]
    slab = lax.axis_index("cross")
    total = jnp.sum(sums[...], axis=0)
    moment = [
        jnp.broadcast_to(jnp.sum(total[i : i + 1], axis=1, keepdims=True), (blocks, width))
        for i in range(2 * ITERS)
    ]
    vel, res = cg_coefficients(moment)
    own = (k0, k1, k2, k3)
    for comp in range(3):
        velocity[comp] = mixed(vel, [k[comp] for k in own[:ITERS]])
        residual[comp] = mixed(res, [k[comp] for k in own])
    lower = picked_beads((d0, d1, d2), vel, dn_plane[3, 1:2, :], slab > 0)
    upper = picked_beads(
        (u0, u1, u2), vel, up_plane[3, 0:1, :], slab < lax.axis_size("cross") - 1
    )
    for comp in range(3):
        arrivals[comp] = lower[comp] + upper[comp]


def finish_call(sums, own, below, above, planes):
    blocks, width = own[1].shape[1:]
    vmem = pl.BlockSpec(memory_space=pltpu.VMEM)
    field = jax.ShapeDtypeStruct((3, blocks, width), jnp.float32)
    return pl.pallas_call(
        finish_kernel,
        in_specs=[vmem] * 13,
        out_specs=[vmem] * 3,
        out_shape=[field, field, jax.ShapeDtypeStruct((3, 1, width), jnp.float32)],
        compiler_params=pltpu.CompilerParams(vmem_limit_bytes=4 << 20),
    )(sums, *own, *below, *above, *planes)


def stage_kernel(tiles, drag, force, tiles_out, drag_out, force_out, sems):
    copies = [
        pltpu.make_async_copy(source, target, sems.at[i])
        for i, (source, target) in enumerate(
            ((tiles, tiles_out), (drag, drag_out), (force, force_out))
        )
    ]
    for copy in copies:
        copy.start()
    for copy in copies:
        copy.wait()


def stage_call(tiles, drag, force):
    arrays = (tiles, drag, force)
    return pl.pallas_call(
        stage_kernel,
        in_specs=[pl.BlockSpec(memory_space=pltpu.HBM)] * 3,
        out_specs=[pl.BlockSpec(memory_space=pltpu.VMEM)] * 3,
        out_shape=[jax.ShapeDtypeStruct(a.shape, a.dtype) for a in arrays],
        scratch_shapes=[pltpu.SemaphoreType.DMA((3,))],
        compiler_params=pltpu.CompilerParams(vmem_limit_bytes=4 << 20),
        cost_estimate=pl.CostEstimate(flops=0, bytes_accessed=2 * tiles.size * 2, transcendentals=0),
    )(*arrays)


def leaving_rows(mig_rows, mig_count, blocks, width):
    capacity = mig_rows.shape[-1]
    live = lax.broadcasted_iota(jnp.int32, (2, capacity), 1) < mig_count[0, 0][:, None]
    rows = jnp.where(live, mig_rows[0, 0], -1).astype(jnp.float32)
    none = jnp.full((1, width - capacity), -1.0, jnp.float32)
    to_lower = jnp.concatenate([none, rows[0:1]], axis=1)
    to_upper = jnp.concatenate([rows[1:2], none], axis=1)
    rest = jnp.zeros((blocks - 2, width), jnp.float32)
    return jnp.concatenate([to_lower, to_upper, rest], axis=0)


def spread_sum(part, axis):
    count = lax.axis_size(axis)
    copies = jnp.broadcast_to(part[None], (count,) + part.shape)
    return lax.all_to_all(copies, axis, 0, 0)


def on_device(force, self_drag, tiles, tile_ids, mig_rows, mig_count):
    field = jnp.swapaxes(force[0, 0], 0, 1)
    drag = self_drag[0, 0]
    blocks, width = drag.shape
    ids = tile_ids[0, 0]
    slab = lax.axis_index("cross")
    last = lax.axis_size("cross") - 1
    carried = leaving_rows(mig_rows, mig_count, blocks, width)
    now = field
    held, drag, field = stage_call(tiles[0, 0], drag, field)
    own, below, above, planes = [], [], [], []
    for sweep in range(ITERS):
        cross_dn = ring_shift(now, "cross", 1)
        cross_up = ring_shift(now, "cross", -1)
        axial_dn = ring_shift(now, "axial", 1)
        axial_up = ring_shift(now, "axial", -1)
        now = field if sweep == 0 else now
        own.append(now)
        below.append(cross_dn)
        above.append(cross_up)
        r1, r3, r5, r7, kept, carried = operator_call(
            sweep, ids, (now, axial_dn, cross_dn, cross_up, axial_up), held, drag, carried
        )
        from_lower_axial = ring_shift(r7, "axial", 1)
        from_upper_axial = ring_shift(r1, "axial", -1)
        if sweep == ITERS - 1:
            part = jnp.sum(spread_sum(carried, "axial"), axis=0)
            part, r3, r5 = lax.optimization_barrier((part, r3, r5))
            part, from_lower_axial, from_upper_axial = lax.optimization_barrier(
                (part, from_lower_axial, from_upper_axial)
            )
            sums = spread_sum(part, "cross")
        from_lower_cross = ring_shift(r5, "cross", 1)
        from_upper_cross = ring_shift(r3, "cross", -1)
        if sweep == 0:
            planes = [from_lower_cross, from_upper_cross]
        now = kept + from_lower_axial + from_upper_axial
        now = now + jnp.where(slab > 0, from_lower_cross[:3], 0.0)
        now = now + jnp.where(slab < last, from_upper_cross[:3], 0.0)
    own.append(now)
    velocity, residual, arrivals = finish_call(sums, own, below, above, planes)
    return (
        jnp.swapaxes(velocity, 0, 1)[None, None],
        jnp.swapaxes(residual, 0, 1)[None, None],
        jnp.swapaxes(arrivals, 0, 1)[None],
    )


def solution(mesh):
    placed = (
        P("axial", "cross", None, None, None),
        P("axial", "cross", None, None),
        P("axial", "cross", None, None, None, None),
        P("axial", "cross", None, None),
        P("axial", "cross", None, None),
        P("axial", "cross", None),
    )
    return jax.shard_map(
        on_device,
        mesh=mesh,
        in_specs=placed,
        out_specs=(
            P("axial", "cross", None, None, None),
            P("axial", "cross", None, None, None),
            P("axial", "cross", None, None),
        ),
        check_vma=False,
    )
```

```python
import functools

import jax
import jax.numpy as jnp
from jax import lax
from jax.experimental import pallas as pl
from jax.experimental.pallas import tpu as pltpu
from jax.sharding import PartitionSpec as P

ITERS = 3
PLACES = (1, 3, 4, 5, 7)
SUB = 8
LOW = 4


def ring(count, by):
    return [(i, (i + by) % count) for i in range(count)]


def ring_shift(shard, axis, by):
    return lax.ppermute(shard, axis, ring(lax.axis_size(axis), by))


def high_low(x):
    high = x.astype(jnp.bfloat16).astype(jnp.float32)
    return high, x - high


def operator_kernel(
    sweep, ids, own, from_axial_dn, from_cross_dn, from_cross_up, from_axial_up, tiles, drag, carried,
    to_axial_dn, to_cross_dn, to_cross_up, to_axial_up, kept, moments, ext, acc,
):
    blocks, count = ids.shape
    width = tiles.shape[-1]
    slab = lax.axis_index("cross")
    has_dn = jnp.where(slab > 0, 1.0, 0.0).astype(jnp.float32)
    has_up = jnp.where(slab < lax.axis_size("cross") - 1, 1.0, 0.0).astype(jnp.float32)
    sources = (from_axial_dn, from_cross_dn, own, from_cross_up, from_axial_up)
    blank = jnp.zeros((blocks, width), jnp.float32)
    for place, source in zip(PLACES, sources):
        base = place * blocks * SUB
        for comp in range(3):
            x = source[comp]
            if place == 3:
                x = x * has_dn
            if place == 5:
                x = x * has_up
            high, low = high_low(x)
            ext[pl.ds(base + comp, blocks, stride=SUB), :] = high
            ext[pl.ds(base + LOW + comp, blocks, stride=SUB), :] = low
        ext[pl.ds(base + 3, blocks, stride=SUB), :] = blank
        ext[pl.ds(base + LOW + 3, blocks, stride=SUB), :] = blank
    acc[...] = jnp.zeros_like(acc)
    rows = lax.broadcasted_iota(jnp.int32, (SUB, width), 0)
    squares = jnp.zeros((SUB, width), jnp.float32)
    for b in range(blocks):
        starts = [pl.multiple_of(ids[b, k] * SUB, SUB) for k in range(count)]
        coupled = jnp.zeros((SUB, width), jnp.float32)
        for k in range(0, count, 2):
            picked = jnp.concatenate(
                [ext[pl.ds(starts[k], SUB), :], ext[pl.ds(starts[k + 1], SUB), :]], axis=1
            ).astype(jnp.bfloat16)
            pair = jnp.concatenate([tiles[b, k], tiles[b, k + 1]], axis=1)
            coupled += lax.dot_general(
                picked, pair, (((1,), (1,)), ((), ())), preferred_element_type=jnp.float32
            )
        coupled = coupled + pltpu.roll(coupled, LOW, 0)
        squares += jnp.where(rows < LOW, coupled * coupled, 0.0)
        high, low = high_low(coupled)
        parts = jnp.where(rows < LOW, high, low).astype(jnp.bfloat16)
        for k in range(count):
            acc[pl.ds(starts[k], SUB), :] += jnp.dot(
                parts, tiles[b, k], preferred_element_type=jnp.float32
            )
    targets = (to_axial_dn, to_cross_dn, None, to_cross_up, to_axial_up)
    even = jnp.zeros((blocks, width), jnp.float32)
    odd = squares
    for place, target in zip(PLACES, targets):
        base = place * blocks * SUB
        for comp in range(3):
            total = (
                acc[pl.ds(base + comp, blocks, stride=SUB), :]
                + acc[pl.ds(base + LOW + comp, blocks, stride=SUB), :]
            )
            if target is None:
                x = own[comp]
                dragged = drag[...] * x
                even += x * x
                odd += dragged * x
                kept[comp] = dragged + total
            else:
                target[comp] = total
    even = jnp.sum(even, axis=0, keepdims=True)
    odd = jnp.sum(odd, axis=0, keepdims=True)
    if sweep == 0:
        moments[...] = jnp.where(rows == 0, even, jnp.where(rows == 1, odd, 0.0))
        to_cross_dn[3] = carried[...]
        to_cross_up[3] = carried[...]
    else:
        merged = jnp.where(
            rows == 2 * sweep, even, jnp.where(rows == 2 * sweep + 1, odd, carried[...])
        )
        moments[...] = jnp.broadcast_to(merged, moments.shape)


def operator_call(sweep, ids, sources, tiles, drag, carried, copies):
    blocks, width = drag.shape
    vmem = pl.BlockSpec(memory_space=pltpu.VMEM)
    field = jax.ShapeDtypeStruct((3, blocks, width), jnp.float32)
    across = jax.ShapeDtypeStruct((4 if sweep == 0 else 3, blocks, width), jnp.float32)
    plane = (SUB, width) if copies is None else (copies, SUB, width)
    plane = jax.ShapeDtypeStruct(plane, jnp.float32)
    return pl.pallas_call(
        functools.partial(operator_kernel, sweep),
        in_specs=[pl.BlockSpec(memory_space=pltpu.SMEM)] + [vmem] * 8,
        out_specs=[vmem] * 6,
        out_shape=[field, across, across, field, field, plane],
        scratch_shapes=[
            pltpu.VMEM((8 * blocks * SUB, width), jnp.float32),
            pltpu.VMEM((8 * blocks * SUB, width), jnp.float32),
        ],
        compiler_params=pltpu.CompilerParams(vmem_limit_bytes=4 << 20),
    )(ids, *sources, tiles, drag, carried)


def shifted_poly(poly):
    return [None] + list(poly)


def combine(left, scale, right):
    out = []
    for i in range(max(len(left), len(right))):
        a = left[i] if i < len(left) else None
        b = right[i] if i < len(right) else None
        b = None if b is None else scale * b
        out.append(b if a is None else a if b is None else a + b)
    return out


def inner(left, right, shift, moment):
    total = None
    for i, a in enumerate(left):
        for j, b in enumerate(right):
            term = a * b * moment[i + j + shift]
            total = term if total is None else total + term
    return total


def cg_coefficients(moment):
    one = jnp.ones_like(moment[0])
    velocity, residual, direction = [], [one], [one]
    norm_now = moment[0]
    for sweep in range(ITERS):
        alpha = norm_now / inner(direction, direction, 1, moment)
        velocity = combine(velocity, alpha, direction)
        residual = combine(residual, -alpha, shifted_poly(direction))
        if sweep < ITERS - 1:
            norm_next = inner(residual, residual, 0, moment)
            direction = combine(residual, norm_next / norm_now, direction)
            norm_now = norm_next
    return velocity, residual


def mixed(coefs, fields):
    total = coefs[0] * fields[0]
    for c, f in zip(coefs[1:], fields[1:]):
        total = total + c * f
    return total


def picked_beads(fields, coefs, wanted, live):
    blocks, width = fields[0][0].shape
    index = jnp.where(live, wanted.astype(jnp.int32), -1)
    block = lax.shift_right_arithmetic(index, 7)
    place = jnp.bitwise_and(index, width - 1)
    parts = []
    for comp in range(3):
        x = mixed(coefs, [f[comp] for f in fields])
        high, rest = high_low(x)
        middle, low = high_low(rest)
        parts += [high, middle, low]
    stacked = jnp.concatenate(parts + [jnp.zeros_like(parts[0])], axis=0).astype(jnp.bfloat16)
    lanes = lax.broadcasted_iota(jnp.int32, (width, width), 0)
    chosen = jnp.where(lanes == place, 1.0, 0.0).astype(jnp.bfloat16)
    found = jnp.dot(stacked, chosen, preferred_element_type=jnp.float32)
    keep = lax.broadcasted_iota(jnp.int32, (blocks, width), 0) == block
    out = []
    for comp in range(3):
        at = 3 * comp * blocks
        x = (
            found[at : at + blocks]
            + found[at + blocks : at + 2 * blocks]
            + found[at + 2 * blocks : at + 3 * blocks]
        )
        out.append(jnp.sum(jnp.where(keep, x, 0.0), axis=0, keepdims=True))
    return out


def finish_kernel(
    sums, k0, k1, k2, k3, d0, d1, d2, u0, u1, u2, dn_plane, up_plane, velocity, residual, arrivals
):
    blocks, width = k0.shape[1:]
    slab = lax.axis_index("cross")
    total = jnp.sum(sums[...], axis=0)
    moment = [
        jnp.broadcast_to(jnp.sum(total[i : i + 1], axis=1, keepdims=True), (blocks, width))
        for i in range(2 * ITERS)
    ]
    vel, res = cg_coefficients(moment)
    own = (k0, k1, k2, k3)
    for comp in range(3):
        velocity[comp] = mixed(vel, [k[comp] for k in own[:ITERS]])
        residual[comp] = mixed(res, [k[comp] for k in own])
    lower = picked_beads((d0, d1, d2), vel, dn_plane[3, 1:2, :], slab > 0)
    upper = picked_beads(
        (u0, u1, u2), vel, up_plane[3, 0:1, :], slab < lax.axis_size("cross") - 1
    )
    for comp in range(3):
        arrivals[comp] = lower[comp] + upper[comp]


def finish_call(sums, own, below, above, planes):
    blocks, width = own[1].shape[1:]
    vmem = pl.BlockSpec(memory_space=pltpu.VMEM)
    field = jax.ShapeDtypeStruct((3, blocks, width), jnp.float32)
    return pl.pallas_call(
        finish_kernel,
        in_specs=[vmem] * 13,
        out_specs=[vmem] * 3,
        out_shape=[field, field, jax.ShapeDtypeStruct((3, 1, width), jnp.float32)],
        compiler_params=pltpu.CompilerParams(vmem_limit_bytes=4 << 20),
    )(sums, *own, *below, *above, *planes)


def stage_kernel(tiles, drag, force, tiles_out, drag_out, force_out, sems):
    copies = [
        pltpu.make_async_copy(source, target, sems.at[i])
        for i, (source, target) in enumerate(
            ((tiles, tiles_out), (drag, drag_out), (force, force_out))
        )
    ]
    for copy in copies:
        copy.start()
    for copy in copies:
        copy.wait()


def stage_call(tiles, drag, force):
    arrays = (tiles, drag, force)
    return pl.pallas_call(
        stage_kernel,
        in_specs=[pl.BlockSpec(memory_space=pltpu.HBM)] * 3,
        out_specs=[pl.BlockSpec(memory_space=pltpu.VMEM)] * 3,
        out_shape=[jax.ShapeDtypeStruct(a.shape, a.dtype) for a in arrays],
        scratch_shapes=[pltpu.SemaphoreType.DMA((3,))],
        compiler_params=pltpu.CompilerParams(vmem_limit_bytes=4 << 20),
        cost_estimate=pl.CostEstimate(flops=0, bytes_accessed=2 * tiles.size * 2, transcendentals=0),
    )(*arrays)


def leaving_rows(mig_rows, mig_count, blocks, width):
    capacity = mig_rows.shape[-1]
    live = lax.broadcasted_iota(jnp.int32, (2, capacity), 1) < mig_count[0, 0][:, None]
    rows = jnp.where(live, mig_rows[0, 0], -1).astype(jnp.float32)
    none = jnp.full((1, width - capacity), -1.0, jnp.float32)
    to_lower = jnp.concatenate([none, rows[0:1]], axis=1)
    to_upper = jnp.concatenate([rows[1:2], none], axis=1)
    rest = jnp.zeros((blocks - 2, width), jnp.float32)
    return jnp.concatenate([to_lower, to_upper, rest], axis=0)


def spread_sum(part, key):
    axial, cross = lax.axis_size("axial"), lax.axis_size("cross")
    groups = {}
    for a in range(axial):
        for c in range(cross):
            groups.setdefault(key(a, c), []).append(a * cross + c)
    groups = list(groups.values())
    if part.ndim == 2:
        part = jnp.broadcast_to(part[None], (len(groups[0]),) + part.shape)
    return lax.all_to_all(part, ("axial", "cross"), 0, 0, axis_index_groups=groups)


def on_device(force, self_drag, tiles, tile_ids, mig_rows, mig_count):
    field = jnp.swapaxes(force[0, 0], 0, 1)
    drag = self_drag[0, 0]
    blocks, width = drag.shape
    ids = tile_ids[0, 0]
    slab = lax.axis_index("cross")
    last = lax.axis_size("cross") - 1
    carried = leaving_rows(mig_rows, mig_count, blocks, width)
    now = field
    held, drag, field = stage_call(tiles[0, 0], drag, field)
    own, below, above, planes = [], [], [], []
    for sweep in range(ITERS):
        cross_dn = ring_shift(now, "cross", 1)
        cross_up = ring_shift(now, "cross", -1)
        axial_dn = ring_shift(now, "axial", 1)
        axial_up = ring_shift(now, "axial", -1)
        now = field if sweep == 0 else now
        own.append(now)
        below.append(cross_dn)
        above.append(cross_up)
        r1, r3, r5, r7, kept, carried = operator_call(
            sweep, ids, (now, axial_dn, cross_dn, cross_up, axial_up), held, drag, carried,
            2 * lax.axis_size("axial") if sweep == ITERS - 1 else None,
        )
        if sweep == ITERS - 1:
            part = jnp.sum(spread_sum(carried, lambda a, c: c // 2), axis=0)
            part, r1, r7 = lax.optimization_barrier((part, r1, r7))
        from_lower_cross = ring_shift(r5, "cross", 1)
        from_upper_cross = ring_shift(r3, "cross", -1)
        if sweep == ITERS - 1:
            part, from_lower_cross, from_upper_cross = lax.optimization_barrier(
                (part, from_lower_cross, from_upper_cross)
            )
            sums = spread_sum(part, lambda a, c: (a, c % 2))
        from_lower_axial = ring_shift(r7, "axial", 1)
        from_upper_axial = ring_shift(r1, "axial", -1)
        if sweep == 0:
            planes = [from_lower_cross, from_upper_cross]
        now = kept + from_lower_axial + from_upper_axial
        now = now + jnp.where(slab > 0, from_lower_cross[:3], 0.0)
        now = now + jnp.where(slab < last, from_upper_cross[:3], 0.0)
    own.append(now)
    velocity, residual, arrivals = finish_call(sums, own, below, above, planes)
    return (
        jnp.swapaxes(velocity, 0, 1)[None, None],
        jnp.swapaxes(residual, 0, 1)[None, None],
        jnp.swapaxes(arrivals, 0, 1)[None],
    )


def solution(mesh):
    placed = (
        P("axial", "cross", None, None, None),
        P("axial", "cross", None, None),
        P("axial", "cross", None, None, None, None),
        P("axial", "cross", None, None),
        P("axial", "cross", None, None),
        P("axial", "cross", None),
    )
    return jax.shard_map(
        on_device,
        mesh=mesh,
        in_specs=placed,
        out_specs=(
            P("axial", "cross", None, None, None),
            P("axial", "cross", None, None, None),
            P("axial", "cross", None, None),
        ),
        check_vma=False,
    )
```

```python
import functools

import jax
import jax.numpy as jnp
from jax import lax
from jax.experimental import pallas as pl
from jax.experimental.pallas import tpu as pltpu
from jax.sharding import PartitionSpec as P

ITERS = 3
PLACES = (1, 3, 4, 5, 7)
SUB = 8
LOW = 4


def ring(count, by):
    return [(i, (i + by) % count) for i in range(count)]


def ring_shift(shard, axis, by):
    return lax.ppermute(shard, axis, ring(lax.axis_size(axis), by))


def high_low(x):
    high = x.astype(jnp.bfloat16).astype(jnp.float32)
    return high, x - high


def operator_kernel(
    sweep, ids, own, from_axial_dn, from_cross_dn, from_cross_up, from_axial_up, tiles, drag, carried,
    to_axial_dn, to_cross_dn, to_cross_up, to_axial_up, kept, moments, ext, acc,
):
    blocks, count = ids.shape
    width = tiles.shape[-1]
    slab = lax.axis_index("cross")
    has_dn = jnp.where(slab > 0, 1.0, 0.0).astype(jnp.float32)
    has_up = jnp.where(slab < lax.axis_size("cross") - 1, 1.0, 0.0).astype(jnp.float32)
    sources = (from_axial_dn, from_cross_dn, own, from_cross_up, from_axial_up)
    blank = jnp.zeros((blocks, width), jnp.float32)
    for place, source in zip(PLACES, sources):
        base = place * blocks * SUB
        for comp in range(3):
            x = source[comp]
            if place == 3:
                x = x * has_dn
            if place == 5:
                x = x * has_up
            high, low = high_low(x)
            ext[pl.ds(base + comp, blocks, stride=SUB), :] = high
            ext[pl.ds(base + LOW + comp, blocks, stride=SUB), :] = low
        ext[pl.ds(base + 3, blocks, stride=SUB), :] = blank
        ext[pl.ds(base + LOW + 3, blocks, stride=SUB), :] = blank
    acc[...] = jnp.zeros_like(acc)
    rows = lax.broadcasted_iota(jnp.int32, (SUB, width), 0)
    squares = jnp.zeros((SUB, width), jnp.float32)
    for b in range(blocks):
        starts = [pl.multiple_of(ids[b, k] * SUB, SUB) for k in range(count)]
        coupled = jnp.zeros((SUB, width), jnp.float32)
        for k in range(0, count, 2):
            picked = jnp.concatenate(
                [ext[pl.ds(starts[k], SUB), :], ext[pl.ds(starts[k + 1], SUB), :]], axis=1
            ).astype(jnp.bfloat16)
            pair = jnp.concatenate([tiles[b, k], tiles[b, k + 1]], axis=1)
            coupled += lax.dot_general(
                picked, pair, (((1,), (1,)), ((), ())), preferred_element_type=jnp.float32
            )
        coupled = coupled + pltpu.roll(coupled, LOW, 0)
        squares += jnp.where(rows < LOW, coupled * coupled, 0.0)
        high, low = high_low(coupled)
        parts = jnp.where(rows < LOW, high, low).astype(jnp.bfloat16)
        for k in range(count):
            acc[pl.ds(starts[k], SUB), :] += jnp.dot(
                parts, tiles[b, k], preferred_element_type=jnp.float32
            )
    targets = (to_axial_dn, to_cross_dn, None, to_cross_up, to_axial_up)
    even = jnp.zeros((blocks, width), jnp.float32)
    odd = squares
    for place, target in zip(PLACES, targets):
        base = place * blocks * SUB
        for comp in range(3):
            total = (
                acc[pl.ds(base + comp, blocks, stride=SUB), :]
                + acc[pl.ds(base + LOW + comp, blocks, stride=SUB), :]
            )
            if target is None:
                x = own[comp]
                dragged = drag[...] * x
                even += x * x
                odd += dragged * x
                kept[comp] = dragged + total
            else:
                target[comp] = total
    even = jnp.sum(even, axis=0, keepdims=True)
    odd = jnp.sum(odd, axis=0, keepdims=True)
    if sweep == 0:
        moments[...] = jnp.where(rows == 0, even, jnp.where(rows == 1, odd, 0.0))
        to_cross_dn[3] = carried[...]
        to_cross_up[3] = carried[...]
    else:
        merged = jnp.where(
            rows == 2 * sweep, even, jnp.where(rows == 2 * sweep + 1, odd, carried[...])
        )
        moments[...] = jnp.broadcast_to(merged, moments.shape)


def operator_call(sweep, ids, sources, tiles, drag, carried, copies):
    blocks, width = drag.shape
    vmem = pl.BlockSpec(memory_space=pltpu.VMEM)
    field = jax.ShapeDtypeStruct((3, blocks, width), jnp.float32)
    across = jax.ShapeDtypeStruct((4 if sweep == 0 else 3, blocks, width), jnp.float32)
    plane = (SUB, width) if copies is None else (copies, SUB, width)
    plane = jax.ShapeDtypeStruct(plane, jnp.float32)
    return pl.pallas_call(
        functools.partial(operator_kernel, sweep),
        in_specs=[pl.BlockSpec(memory_space=pltpu.SMEM)] + [vmem] * 8,
        out_specs=[vmem] * 6,
        out_shape=[field, across, across, field, field, plane],
        scratch_shapes=[
            pltpu.VMEM((8 * blocks * SUB, width), jnp.float32),
            pltpu.VMEM((8 * blocks * SUB, width), jnp.float32),
        ],
        compiler_params=pltpu.CompilerParams(vmem_limit_bytes=4 << 20),
    )(ids, *sources, tiles, drag, carried)


def shifted_poly(poly):
    return [None] + list(poly)


def combine(left, scale, right):
    out = []
    for i in range(max(len(left), len(right))):
        a = left[i] if i < len(left) else None
        b = right[i] if i < len(right) else None
        b = None if b is None else scale * b
        out.append(b if a is None else a if b is None else a + b)
    return out


def inner(left, right, shift, moment):
    total = None
    for i, a in enumerate(left):
        for j, b in enumerate(right):
            term = a * b * moment[i + j + shift]
            total = term if total is None else total + term
    return total


def cg_coefficients(moment):
    one = jnp.ones_like(moment[0])
    velocity, residual, direction = [], [one], [one]
    norm_now = moment[0]
    for sweep in range(ITERS):
        alpha = norm_now / inner(direction, direction, 1, moment)
        velocity = combine(velocity, alpha, direction)
        residual = combine(residual, -alpha, shifted_poly(direction))
        if sweep < ITERS - 1:
            norm_next = inner(residual, residual, 0, moment)
            direction = combine(residual, norm_next / norm_now, direction)
            norm_now = norm_next
    return velocity, residual


def mixed(coefs, fields):
    total = coefs[0] * fields[0]
    for c, f in zip(coefs[1:], fields[1:]):
        total = total + c * f
    return total


def picked_beads(fields, coefs, wanted, live):
    blocks, width = fields[0][0].shape
    index = jnp.where(live, wanted.astype(jnp.int32), -1)
    block = lax.shift_right_arithmetic(index, 7)
    place = jnp.bitwise_and(index, width - 1)
    parts = []
    for comp in range(3):
        x = mixed(coefs, [f[comp] for f in fields])
        high, rest = high_low(x)
        middle, low = high_low(rest)
        parts += [high, middle, low]
    stacked = jnp.concatenate(parts + [jnp.zeros_like(parts[0])], axis=0).astype(jnp.bfloat16)
    lanes = lax.broadcasted_iota(jnp.int32, (width, width), 0)
    chosen = jnp.where(lanes == place, 1.0, 0.0).astype(jnp.bfloat16)
    found = jnp.dot(stacked, chosen, preferred_element_type=jnp.float32)
    keep = lax.broadcasted_iota(jnp.int32, (blocks, width), 0) == block
    out = []
    for comp in range(3):
        at = 3 * comp * blocks
        x = (
            found[at : at + blocks]
            + found[at + blocks : at + 2 * blocks]
            + found[at + 2 * blocks : at + 3 * blocks]
        )
        out.append(jnp.sum(jnp.where(keep, x, 0.0), axis=0, keepdims=True))
    return out


def finish_kernel(
    sums, k0, k1, k2, k3, d0, d1, d2, u0, u1, u2, dn_plane, up_plane, velocity, residual, arrivals
):
    blocks, width = k0.shape[1:]
    slab = lax.axis_index("cross")
    total = jnp.sum(sums[...], axis=0)
    moment = [
        jnp.broadcast_to(jnp.sum(total[i : i + 1], axis=1, keepdims=True), (blocks, width))
        for i in range(2 * ITERS)
    ]
    vel, res = cg_coefficients(moment)
    own = (k0, k1, k2, k3)
    for comp in range(3):
        velocity[comp] = mixed(vel, [k[comp] for k in own[:ITERS]])
        residual[comp] = mixed(res, [k[comp] for k in own])
    lower = picked_beads((d0, d1, d2), vel, dn_plane[3, 1:2, :], slab > 0)
    upper = picked_beads(
        (u0, u1, u2), vel, up_plane[3, 0:1, :], slab < lax.axis_size("cross") - 1
    )
    for comp in range(3):
        arrivals[comp] = lower[comp] + upper[comp]


def finish_call(sums, own, below, above, planes):
    blocks, width = own[1].shape[1:]
    vmem = pl.BlockSpec(memory_space=pltpu.VMEM)
    field = jax.ShapeDtypeStruct((3, blocks, width), jnp.float32)
    return pl.pallas_call(
        finish_kernel,
        in_specs=[vmem] * 13,
        out_specs=[vmem] * 3,
        out_shape=[field, field, jax.ShapeDtypeStruct((3, 1, width), jnp.float32)],
        compiler_params=pltpu.CompilerParams(vmem_limit_bytes=4 << 20),
    )(sums, *own, *below, *above, *planes)


def stage_kernel(tiles, drag, force, tiles_out, drag_out, force_out, sems):
    copies = [
        pltpu.make_async_copy(source, target, sems.at[i])
        for i, (source, target) in enumerate(
            ((tiles, tiles_out), (drag, drag_out), (force, force_out))
        )
    ]
    for copy in copies:
        copy.start()
    for copy in copies:
        copy.wait()


def stage_call(tiles, drag, force):
    arrays = (tiles, drag, force)
    return pl.pallas_call(
        stage_kernel,
        in_specs=[pl.BlockSpec(memory_space=pltpu.HBM)] * 3,
        out_specs=[pl.BlockSpec(memory_space=pltpu.VMEM)] * 3,
        out_shape=[jax.ShapeDtypeStruct(a.shape, a.dtype) for a in arrays],
        scratch_shapes=[pltpu.SemaphoreType.DMA((3,))],
        compiler_params=pltpu.CompilerParams(vmem_limit_bytes=4 << 20),
        cost_estimate=pl.CostEstimate(flops=0, bytes_accessed=2 * tiles.size * 2, transcendentals=0),
    )(*arrays)


def leaving_rows(mig_rows, mig_count, blocks, width):
    capacity = mig_rows.shape[-1]
    live = lax.broadcasted_iota(jnp.int32, (2, capacity), 1) < mig_count[0, 0][:, None]
    rows = jnp.where(live, mig_rows[0, 0], -1).astype(jnp.float32)
    none = jnp.full((1, width - capacity), -1.0, jnp.float32)
    to_lower = jnp.concatenate([none, rows[0:1]], axis=1)
    to_upper = jnp.concatenate([rows[1:2], none], axis=1)
    rest = jnp.zeros((blocks - 2, width), jnp.float32)
    return jnp.concatenate([to_lower, to_upper, rest], axis=0)


def spread_sum(part, key):
    axial, cross = lax.axis_size("axial"), lax.axis_size("cross")
    groups = {}
    for a in range(axial):
        for c in range(cross):
            groups.setdefault(key(a, c), []).append(a * cross + c)
    groups = list(groups.values())
    if part.ndim == 2:
        part = jnp.broadcast_to(part[None], (len(groups[0]),) + part.shape)
    return lax.all_to_all(part, ("axial", "cross"), 0, 0, axis_index_groups=groups)


def on_device(force, self_drag, tiles, tile_ids, mig_rows, mig_count):
    field = jnp.swapaxes(force[0, 0], 0, 1)
    drag = self_drag[0, 0]
    blocks, width = drag.shape
    ids = tile_ids[0, 0]
    slab = lax.axis_index("cross")
    last = lax.axis_size("cross") - 1
    carried = leaving_rows(mig_rows, mig_count, blocks, width)
    now = field
    held, drag, field = stage_call(tiles[0, 0], drag, field)
    own, below, above, planes = [], [], [], []
    for sweep in range(ITERS):
        cross_dn = ring_shift(now, "cross", 1)
        cross_up = ring_shift(now, "cross", -1)
        axial_dn = ring_shift(now, "axial", 1)
        axial_up = ring_shift(now, "axial", -1)
        now = field if sweep == 0 else now
        own.append(now)
        below.append(cross_dn)
        above.append(cross_up)
        r1, r3, r5, r7, kept, carried = operator_call(
            sweep, ids, (now, axial_dn, cross_dn, cross_up, axial_up), held, drag, carried,
            2 * lax.axis_size("axial") if sweep == ITERS - 1 else None,
        )
        if sweep == ITERS - 1:
            part = jnp.sum(spread_sum(carried, lambda a, c: c // 2), axis=0)
            part, r1, r3, r5, r7 = lax.optimization_barrier((part, r1, r3, r5, r7))
            sums = spread_sum(part, lambda a, c: (a, c % 2))
        from_lower_cross = ring_shift(r5, "cross", 1)
        from_upper_cross = ring_shift(r3, "cross", -1)
        from_lower_axial = ring_shift(r7, "axial", 1)
        from_upper_axial = ring_shift(r1, "axial", -1)
        if sweep == 0:
            planes = [from_lower_cross, from_upper_cross]
        now = kept + from_lower_axial + from_upper_axial
        now = now + jnp.where(slab > 0, from_lower_cross[:3], 0.0)
        now = now + jnp.where(slab < last, from_upper_cross[:3], 0.0)
    own.append(now)
    velocity, residual, arrivals = finish_call(sums, own, below, above, planes)
    return (
        jnp.swapaxes(velocity, 0, 1)[None, None],
        jnp.swapaxes(residual, 0, 1)[None, None],
        jnp.swapaxes(arrivals, 0, 1)[None],
    )


def solution(mesh):
    placed = (
        P("axial", "cross", None, None, None),
        P("axial", "cross", None, None),
        P("axial", "cross", None, None, None, None),
        P("axial", "cross", None, None),
        P("axial", "cross", None, None),
        P("axial", "cross", None),
    )
    return jax.shard_map(
        on_device,
        mesh=mesh,
        in_specs=placed,
        out_specs=(
            P("axial", "cross", None, None, None),
            P("axial", "cross", None, None, None),
            P("axial", "cross", None, None),
        ),
        check_vma=False,
    )
```

```python
import functools

import jax
import jax.numpy as jnp
from jax import lax
from jax.experimental import pallas as pl
from jax.experimental.pallas import tpu as pltpu
from jax.sharding import PartitionSpec as P

ITERS = 3
PLACES = (1, 3, 4, 5, 7)
SUB = 8
LOW = 4


def ring(count, by):
    return [(i, (i + by) % count) for i in range(count)]


def ring_shift(shard, axis, by):
    return lax.ppermute(shard, axis, ring(lax.axis_size(axis), by))


def high_low(x):
    high = x.astype(jnp.bfloat16).astype(jnp.float32)
    return high, x - high


def operator_kernel(
    sweep, own, from_axial_dn, from_cross_dn, from_cross_up, from_axial_up, tiles, drag,
    picker, adder, carried,
    to_axial_dn, to_cross_dn, to_cross_up, to_axial_up, kept, moments, products,
):
    blocks, count, width = tiles.shape[0], tiles.shape[1], tiles.shape[3]
    slab = lax.axis_index("cross")
    has_dn = jnp.where(slab > 0, 1.0, 0.0).astype(jnp.float32)
    has_up = jnp.where(slab < lax.axis_size("cross") - 1, 1.0, 0.0).astype(jnp.float32)
    sources = (from_axial_dn, from_cross_dn, own, from_cross_up, from_axial_up)
    scales = (None, has_dn, None, has_up, None)
    highs, lows = [], []
    for comp in range(3):
        for source, scale in zip(sources, scales):
            x = source[comp] if scale is None else source[comp] * scale
            high, low = high_low(x)
            highs.append(high)
            lows.append(low)
    spare = picker.shape[1] - 6 * len(PLACES) * blocks
    listed = jnp.concatenate(highs + lows + [jnp.zeros((spare, width), jnp.float32)], axis=0)
    picked = jnp.dot(
        picker[...], listed.astype(jnp.bfloat16), preferred_element_type=jnp.float32
    ).astype(jnp.bfloat16)
    rows = lax.broadcasted_iota(jnp.int32, (SUB, width), 0)
    squares = jnp.zeros((SUB, width), jnp.float32)
    for b in range(blocks):
        coupled = jnp.zeros((SUB, width), jnp.float32)
        for k in range(0, count, 2):
            at = (b * count + k) * SUB
            both = jnp.concatenate([picked[at : at + SUB], picked[at + SUB : at + 2 * SUB]], axis=1)
            pair = jnp.concatenate([tiles[b, k], tiles[b, k + 1]], axis=1)
            coupled += lax.dot_general(
                both, pair, (((1,), (1,)), ((), ())), preferred_element_type=jnp.float32
            )
        coupled = coupled + pltpu.roll(coupled, LOW, 0)
        squares += jnp.where(rows < LOW, coupled * coupled, 0.0)
        high, low = high_low(coupled)
        parts = jnp.where(rows < LOW, high, low).astype(jnp.bfloat16)
        for k in range(count):
            at = (b * count + k) * SUB
            products[at : at + SUB, :] = jnp.dot(
                parts, tiles[b, k], preferred_element_type=jnp.float32
            )
    high, low = high_low(products[...])
    returned = jnp.dot(
        adder[...], high.astype(jnp.bfloat16), preferred_element_type=jnp.float32
    ) + jnp.dot(adder[...], low.astype(jnp.bfloat16), preferred_element_type=jnp.float32)
    targets = (to_axial_dn, to_cross_dn, None, to_cross_up, to_axial_up)
    even = jnp.zeros((blocks, width), jnp.float32)
    odd = squares
    for comp in range(3):
        for place, target in enumerate(targets):
            at = (comp * len(PLACES) + place) * blocks
            total = returned[at : at + blocks]
            if target is None:
                x = own[comp]
                dragged = drag[...] * x
                even += x * x
                odd += dragged * x
                kept[comp] = dragged + total
            else:
                target[comp] = total
    even = jnp.sum(even, axis=0, keepdims=True)
    odd = jnp.sum(odd, axis=0, keepdims=True)
    if sweep == 0:
        moments[...] = jnp.where(rows == 0, even, jnp.where(rows == 1, odd, 0.0))
        to_cross_dn[3] = carried[...]
        to_cross_up[3] = carried[...]
    else:
        merged = jnp.where(
            rows == 2 * sweep, even, jnp.where(rows == 2 * sweep + 1, odd, carried[...])
        )
        moments[...] = jnp.broadcast_to(merged, moments.shape)


def operator_call(sweep, sources, tiles, drag, picker, adder, carried, copies):
    blocks, width = drag.shape
    vmem = pl.BlockSpec(memory_space=pltpu.VMEM)
    field = jax.ShapeDtypeStruct((3, blocks, width), jnp.float32)
    across = jax.ShapeDtypeStruct((4 if sweep == 0 else 3, blocks, width), jnp.float32)
    plane = (SUB, width) if copies is None else (copies, SUB, width)
    plane = jax.ShapeDtypeStruct(plane, jnp.float32)
    return pl.pallas_call(
        functools.partial(operator_kernel, sweep),
        in_specs=[vmem] * 10,
        out_specs=[vmem] * 6,
        out_shape=[field, across, across, field, field, plane],
        scratch_shapes=[pltpu.VMEM((tiles.shape[0] * tiles.shape[1] * SUB, width), jnp.float32)],
        compiler_params=pltpu.CompilerParams(vmem_limit_bytes=4 << 20),
    )(*sources, tiles, drag, picker, adder, carried)


def one_hots(tile_ids, blocks):
    place = tile_ids // blocks
    order = sum((place >= p).astype(jnp.int32) for p in PLACES[1:])
    entry = jnp.repeat((order * blocks + tile_ids % blocks).reshape(-1), SUB)
    row = lax.broadcasted_iota(jnp.int32, entry.shape, 0) % SUB
    comp, listed = row % LOW, len(PLACES) * blocks
    used = comp < 3
    source = jnp.where(used, (comp + 3 * (row // LOW)) * listed + entry, -1)
    target = jnp.where(used, comp * listed + entry, -1)
    wide = -(-6 * listed // 128) * 128
    tall = -(-3 * listed // 16) * 16
    picker = source[:, None] == lax.broadcasted_iota(jnp.int32, (1, wide), 1)
    adder = lax.broadcasted_iota(jnp.int32, (tall, 1), 0) == target[None, :]
    return picker.astype(jnp.bfloat16), adder.astype(jnp.bfloat16)


def shifted_poly(poly):
    return [None] + list(poly)


def combine(left, scale, right):
    out = []
    for i in range(max(len(left), len(right))):
        a = left[i] if i < len(left) else None
        b = right[i] if i < len(right) else None
        b = None if b is None else scale * b
        out.append(b if a is None else a if b is None else a + b)
    return out


def inner(left, right, shift, moment):
    total = None
    for i, a in enumerate(left):
        for j, b in enumerate(right):
            term = a * b * moment[i + j + shift]
            total = term if total is None else total + term
    return total


def cg_coefficients(moment):
    one = jnp.ones_like(moment[0])
    velocity, residual, direction = [], [one], [one]
    norm_now = moment[0]
    for sweep in range(ITERS):
        alpha = norm_now / inner(direction, direction, 1, moment)
        velocity = combine(velocity, alpha, direction)
        residual = combine(residual, -alpha, shifted_poly(direction))
        if sweep < ITERS - 1:
            norm_next = inner(residual, residual, 0, moment)
            direction = combine(residual, norm_next / norm_now, direction)
            norm_now = norm_next
    return velocity, residual


def mixed(coefs, fields):
    total = coefs[0] * fields[0]
    for c, f in zip(coefs[1:], fields[1:]):
        total = total + c * f
    return total


def picked_beads(fields, coefs, wanted, live):
    blocks, width = fields[0][0].shape
    index = jnp.where(live, wanted.astype(jnp.int32), -1)
    block = lax.shift_right_arithmetic(index, 7)
    place = jnp.bitwise_and(index, width - 1)
    parts = []
    for comp in range(3):
        x = mixed(coefs, [f[comp] for f in fields])
        high, rest = high_low(x)
        middle, low = high_low(rest)
        parts += [high, middle, low]
    stacked = jnp.concatenate(parts + [jnp.zeros_like(parts[0])], axis=0).astype(jnp.bfloat16)
    lanes = lax.broadcasted_iota(jnp.int32, (width, width), 0)
    chosen = jnp.where(lanes == place, 1.0, 0.0).astype(jnp.bfloat16)
    found = jnp.dot(stacked, chosen, preferred_element_type=jnp.float32)
    keep = lax.broadcasted_iota(jnp.int32, (blocks, width), 0) == block
    out = []
    for comp in range(3):
        at = 3 * comp * blocks
        x = (
            found[at : at + blocks]
            + found[at + blocks : at + 2 * blocks]
            + found[at + 2 * blocks : at + 3 * blocks]
        )
        out.append(jnp.sum(jnp.where(keep, x, 0.0), axis=0, keepdims=True))
    return out


def finish_kernel(
    sums, k0, k1, k2, k3, d0, d1, d2, u0, u1, u2, dn_plane, up_plane, velocity, residual, arrivals
):
    blocks, width = k0.shape[1:]
    slab = lax.axis_index("cross")
    total = jnp.sum(sums[...], axis=0)
    moment = [
        jnp.broadcast_to(jnp.sum(total[i : i + 1], axis=1, keepdims=True), (blocks, width))
        for i in range(2 * ITERS)
    ]
    vel, res = cg_coefficients(moment)
    own = (k0, k1, k2, k3)
    for comp in range(3):
        velocity[comp] = mixed(vel, [k[comp] for k in own[:ITERS]])
        residual[comp] = mixed(res, [k[comp] for k in own])
    lower = picked_beads((d0, d1, d2), vel, dn_plane[3, 1:2, :], slab > 0)
    upper = picked_beads(
        (u0, u1, u2), vel, up_plane[3, 0:1, :], slab < lax.axis_size("cross") - 1
    )
    for comp in range(3):
        arrivals[comp] = lower[comp] + upper[comp]


def finish_call(sums, own, below, above, planes):
    blocks, width = own[1].shape[1:]
    vmem = pl.BlockSpec(memory_space=pltpu.VMEM)
    field = jax.ShapeDtypeStruct((3, blocks, width), jnp.float32)
    return pl.pallas_call(
        finish_kernel,
        in_specs=[vmem] * 13,
        out_specs=[vmem] * 3,
        out_shape=[field, field, jax.ShapeDtypeStruct((3, 1, width), jnp.float32)],
        compiler_params=pltpu.CompilerParams(vmem_limit_bytes=4 << 20),
    )(sums, *own, *below, *above, *planes)


def stage_kernel(tiles, drag, force, tiles_out, drag_out, force_out, sems):
    copies = [
        pltpu.make_async_copy(source, target, sems.at[i])
        for i, (source, target) in enumerate(
            ((tiles, tiles_out), (drag, drag_out), (force, force_out))
        )
    ]
    for copy in copies:
        copy.start()
    for copy in copies:
        copy.wait()


def stage_call(tiles, drag, force):
    arrays = (tiles, drag, force)
    return pl.pallas_call(
        stage_kernel,
        in_specs=[pl.BlockSpec(memory_space=pltpu.HBM)] * 3,
        out_specs=[pl.BlockSpec(memory_space=pltpu.VMEM)] * 3,
        out_shape=[jax.ShapeDtypeStruct(a.shape, a.dtype) for a in arrays],
        scratch_shapes=[pltpu.SemaphoreType.DMA((3,))],
        compiler_params=pltpu.CompilerParams(vmem_limit_bytes=4 << 20),
        cost_estimate=pl.CostEstimate(flops=0, bytes_accessed=2 * tiles.size * 2, transcendentals=0),
    )(*arrays)


def leaving_rows(mig_rows, mig_count, blocks, width):
    capacity = mig_rows.shape[-1]
    live = lax.broadcasted_iota(jnp.int32, (2, capacity), 1) < mig_count[0, 0][:, None]
    rows = jnp.where(live, mig_rows[0, 0], -1).astype(jnp.float32)
    none = jnp.full((1, width - capacity), -1.0, jnp.float32)
    to_lower = jnp.concatenate([none, rows[0:1]], axis=1)
    to_upper = jnp.concatenate([rows[1:2], none], axis=1)
    rest = jnp.zeros((blocks - 2, width), jnp.float32)
    return jnp.concatenate([to_lower, to_upper, rest], axis=0)


def spread_sum(part, key):
    axial, cross = lax.axis_size("axial"), lax.axis_size("cross")
    groups = {}
    for a in range(axial):
        for c in range(cross):
            groups.setdefault(key(a, c), []).append(a * cross + c)
    groups = list(groups.values())
    if part.ndim == 2:
        part = jnp.broadcast_to(part[None], (len(groups[0]),) + part.shape)
    return lax.all_to_all(part, ("axial", "cross"), 0, 0, axis_index_groups=groups)


def on_device(force, self_drag, tiles, tile_ids, mig_rows, mig_count):
    field = jnp.swapaxes(force[0, 0], 0, 1)
    drag = self_drag[0, 0]
    blocks, width = drag.shape
    picker, adder = one_hots(tile_ids[0, 0], blocks)
    slab = lax.axis_index("cross")
    last = lax.axis_size("cross") - 1
    carried = leaving_rows(mig_rows, mig_count, blocks, width)
    now = field
    held, drag, field = stage_call(tiles[0, 0], drag, field)
    own, below, above, planes = [], [], [], []
    for sweep in range(ITERS):
        cross_dn = ring_shift(now, "cross", 1)
        cross_up = ring_shift(now, "cross", -1)
        axial_dn = ring_shift(now, "axial", 1)
        axial_up = ring_shift(now, "axial", -1)
        now = field if sweep == 0 else now
        own.append(now)
        below.append(cross_dn)
        above.append(cross_up)
        r1, r3, r5, r7, kept, carried = operator_call(
            sweep, (now, axial_dn, cross_dn, cross_up, axial_up), held, drag, picker, adder, carried,
            2 * lax.axis_size("axial") if sweep == ITERS - 1 else None,
        )
        if sweep == ITERS - 1:
            part = jnp.sum(spread_sum(carried, lambda a, c: c // 2), axis=0)
            part, r1, r7 = lax.optimization_barrier((part, r1, r7))
        from_lower_cross = ring_shift(r5, "cross", 1)
        from_upper_cross = ring_shift(r3, "cross", -1)
        if sweep == ITERS - 1:
            part, from_lower_cross, from_upper_cross = lax.optimization_barrier(
                (part, from_lower_cross, from_upper_cross)
            )
            sums = spread_sum(part, lambda a, c: (a, c % 2))
        from_lower_axial = ring_shift(r7, "axial", 1)
        from_upper_axial = ring_shift(r1, "axial", -1)
        if sweep == 0:
            planes = [from_lower_cross, from_upper_cross]
        now = kept + from_lower_axial + from_upper_axial
        now = now + jnp.where(slab > 0, from_lower_cross[:3], 0.0)
        now = now + jnp.where(slab < last, from_upper_cross[:3], 0.0)
    own.append(now)
    velocity, residual, arrivals = finish_call(sums, own, below, above, planes)
    return (
        jnp.swapaxes(velocity, 0, 1)[None, None],
        jnp.swapaxes(residual, 0, 1)[None, None],
        jnp.swapaxes(arrivals, 0, 1)[None],
    )


def solution(mesh):
    placed = (
        P("axial", "cross", None, None, None),
        P("axial", "cross", None, None),
        P("axial", "cross", None, None, None, None),
        P("axial", "cross", None, None),
        P("axial", "cross", None, None),
        P("axial", "cross", None),
    )
    return jax.shard_map(
        on_device,
        mesh=mesh,
        in_specs=placed,
        out_specs=(
            P("axial", "cross", None, None, None),
            P("axial", "cross", None, None, None),
            P("axial", "cross", None, None),
        ),
        check_vma=False,
    )
```

```python
import functools

import jax
import jax.numpy as jnp
from jax import lax
from jax.experimental import pallas as pl
from jax.experimental.pallas import tpu as pltpu
from jax.sharding import PartitionSpec as P

ITERS = 3
PLACES = (1, 3, 4, 5, 7)
SUB = 8
FIRST_EXCHANGE_FLOPS = 8 * 10**9
LOW = 4


def ring(count, by):
    return [(i, (i + by) % count) for i in range(count)]


def ring_shift(shard, axis, by):
    return lax.ppermute(shard, axis, ring(lax.axis_size(axis), by))


def high_low(x):
    high = x.astype(jnp.bfloat16).astype(jnp.float32)
    return high, x - high


def operator_kernel(
    sweep, ids, own, from_axial_dn, from_cross_dn, from_cross_up, from_axial_up, tiles, drag, *rest
):
    many = (1, 2, 1)[sweep]
    carried, rest = rest[:many], rest[many:]
    (
        to_axial_dn, to_cross_dn, to_cross_up, to_axial_up, kept, moments, ext, acc,
    ) = rest
    blocks, count = ids.shape
    width = tiles.shape[-1]
    slab = lax.axis_index("cross")
    has_dn = jnp.where(slab > 0, 1.0, 0.0).astype(jnp.float32)
    has_up = jnp.where(slab < lax.axis_size("cross") - 1, 1.0, 0.0).astype(jnp.float32)
    sources = (from_axial_dn, from_cross_dn, own, from_cross_up, from_axial_up)
    blank = jnp.zeros((blocks, width), jnp.float32)
    for place, source in zip(PLACES, sources):
        base = place * blocks * SUB
        for comp in range(3):
            x = source[comp]
            if place == 3:
                x = x * has_dn
            if place == 5:
                x = x * has_up
            high, low = high_low(x)
            ext[pl.ds(base + comp, blocks, stride=SUB), :] = high
            ext[pl.ds(base + LOW + comp, blocks, stride=SUB), :] = low
        ext[pl.ds(base + 3, blocks, stride=SUB), :] = blank
        ext[pl.ds(base + LOW + 3, blocks, stride=SUB), :] = blank
    acc[...] = jnp.zeros_like(acc)
    rows = lax.broadcasted_iota(jnp.int32, (SUB, width), 0)
    squares = jnp.zeros((SUB, width), jnp.float32)
    for b in range(blocks):
        starts = [pl.multiple_of(ids[b, k] * SUB, SUB) for k in range(count)]
        coupled = jnp.zeros((SUB, width), jnp.float32)
        for k in range(0, count, 2):
            picked = jnp.concatenate(
                [ext[pl.ds(starts[k], SUB), :], ext[pl.ds(starts[k + 1], SUB), :]], axis=1
            ).astype(jnp.bfloat16)
            pair = jnp.concatenate([tiles[b, k], tiles[b, k + 1]], axis=1)
            coupled += lax.dot_general(
                picked, pair, (((1,), (1,)), ((), ())), preferred_element_type=jnp.float32
            )
        coupled = coupled + pltpu.roll(coupled, LOW, 0)
        squares += jnp.where(rows < LOW, coupled * coupled, 0.0)
        high, low = high_low(coupled)
        parts = jnp.where(rows < LOW, high, low).astype(jnp.bfloat16)
        for k in range(count):
            acc[pl.ds(starts[k], SUB), :] += jnp.dot(
                parts, tiles[b, k], preferred_element_type=jnp.float32
            )
    targets = (to_axial_dn, to_cross_dn, None, to_cross_up, to_axial_up)
    even = jnp.zeros((blocks, width), jnp.float32)
    odd = squares
    for place, target in zip(PLACES, targets):
        base = place * blocks * SUB
        for comp in range(3):
            total = (
                acc[pl.ds(base + comp, blocks, stride=SUB), :]
                + acc[pl.ds(base + LOW + comp, blocks, stride=SUB), :]
            )
            if target is None:
                x = own[comp]
                dragged = drag[...] * x
                even += x * x
                odd += dragged * x
                kept[comp] = dragged + total
            else:
                target[comp] = total
    even = jnp.sum(even, axis=0, keepdims=True)
    odd = jnp.sum(odd, axis=0, keepdims=True)
    merged = jnp.where(
        rows == 2 * sweep, even, jnp.where(rows == 2 * sweep + 1, odd, carried[0][...])
    )
    moments[...] = jnp.broadcast_to(merged, moments.shape)
    if sweep == 1:
        to_cross_dn[3] = carried[1][...]
        to_cross_up[3] = carried[1][...]


def operator_call(sweep, ids, sources, tiles, drag, carried, copies):
    blocks, width = drag.shape
    vmem = pl.BlockSpec(memory_space=pltpu.VMEM)
    field = jax.ShapeDtypeStruct((3, blocks, width), jnp.float32)
    across = jax.ShapeDtypeStruct((4 if sweep == 1 else 3, blocks, width), jnp.float32)
    plane = (SUB, width) if copies is None else (copies, SUB, width)
    plane = jax.ShapeDtypeStruct(plane, jnp.float32)
    rows = 8 * blocks * SUB
    scratch = [pltpu.VMEM((rows, width), jnp.float32), pltpu.VMEM((rows, width), jnp.float32)]
    return pl.pallas_call(
        functools.partial(operator_kernel, sweep),
        in_specs=[pl.BlockSpec(memory_space=pltpu.SMEM)]
        + [vmem] * 5
        + [vmem] * (2 + len(carried)),
        out_specs=[vmem] * 6,
        out_shape=[field, across, across, field, field, plane],
        scratch_shapes=scratch,
        compiler_params=pltpu.CompilerParams(vmem_limit_bytes=4 << 20),
    )(ids, *sources, tiles, drag, *carried)


def shifted_poly(poly):
    return [None] + list(poly)


def combine(left, scale, right):
    out = []
    for i in range(max(len(left), len(right))):
        a = left[i] if i < len(left) else None
        b = right[i] if i < len(right) else None
        b = None if b is None else scale * b
        out.append(b if a is None else a if b is None else a + b)
    return out


def inner(left, right, shift, moment):
    total = None
    for i, a in enumerate(left):
        for j, b in enumerate(right):
            term = a * b * moment[i + j + shift]
            total = term if total is None else total + term
    return total


def cg_coefficients(moment):
    one = jnp.ones_like(moment[0])
    velocity, residual, direction = [], [one], [one]
    norm_now = moment[0]
    for sweep in range(ITERS):
        alpha = norm_now / inner(direction, direction, 1, moment)
        velocity = combine(velocity, alpha, direction)
        residual = combine(residual, -alpha, shifted_poly(direction))
        if sweep < ITERS - 1:
            norm_next = inner(residual, residual, 0, moment)
            direction = combine(residual, norm_next / norm_now, direction)
            norm_now = norm_next
    return velocity, residual


def mixed(coefs, fields):
    total = coefs[0] * fields[0]
    for c, f in zip(coefs[1:], fields[1:]):
        total = total + c * f
    return total


def picked_beads(fields, coefs, wanted, live):
    blocks, width = fields[0][0].shape
    index = jnp.where(live, wanted.astype(jnp.int32), -1)
    block = lax.shift_right_arithmetic(index, 7)
    place = jnp.bitwise_and(index, width - 1)
    parts = []
    for comp in range(3):
        x = mixed(coefs, [f[comp] for f in fields])
        high, rest = high_low(x)
        middle, low = high_low(rest)
        parts += [high, middle, low]
    stacked = jnp.concatenate(parts + [jnp.zeros_like(parts[0])], axis=0).astype(jnp.bfloat16)
    lanes = lax.broadcasted_iota(jnp.int32, (width, width), 0)
    chosen = jnp.where(lanes == place, 1.0, 0.0).astype(jnp.bfloat16)
    found = jnp.dot(stacked, chosen, preferred_element_type=jnp.float32)
    keep = lax.broadcasted_iota(jnp.int32, (blocks, width), 0) == block
    out = []
    for comp in range(3):
        at = 3 * comp * blocks
        x = (
            found[at : at + blocks]
            + found[at + blocks : at + 2 * blocks]
            + found[at + 2 * blocks : at + 3 * blocks]
        )
        out.append(jnp.sum(jnp.where(keep, x, 0.0), axis=0, keepdims=True))
    return out


def finish_kernel(
    sums, k0, k1, k2, k3, d0, d1, d2, u0, u1, u2, dn_plane, up_plane, velocity, residual, arrivals
):
    blocks, width = k0.shape[1:]
    slab = lax.axis_index("cross")
    total = jnp.sum(sums[...], axis=0)
    moment = [
        jnp.broadcast_to(jnp.sum(total[i : i + 1], axis=1, keepdims=True), (blocks, width))
        for i in range(2 * ITERS)
    ]
    vel, res = cg_coefficients(moment)
    own = (k0, k1, k2, k3)
    for comp in range(3):
        velocity[comp] = mixed(vel, [k[comp] for k in own[:ITERS]])
        residual[comp] = mixed(res, [k[comp] for k in own])
    lower = picked_beads((d0, d1, d2), vel, dn_plane[3, 1:2, :], slab > 0)
    upper = picked_beads(
        (u0, u1, u2), vel, up_plane[3, 0:1, :], slab < lax.axis_size("cross") - 1
    )
    for comp in range(3):
        arrivals[comp] = lower[comp] + upper[comp]


def finish_call(sums, own, below, above, planes):
    blocks, width = own[1].shape[1:]
    vmem = pl.BlockSpec(memory_space=pltpu.VMEM)
    field = jax.ShapeDtypeStruct((3, blocks, width), jnp.float32)
    return pl.pallas_call(
        finish_kernel,
        in_specs=[vmem] * 13,
        out_specs=[vmem] * 3,
        out_shape=[field, field, jax.ShapeDtypeStruct((3, 1, width), jnp.float32)],
        compiler_params=pltpu.CompilerParams(vmem_limit_bytes=4 << 20),
    )(sums, *own, *below, *above, *planes)


def no_moments_kernel(moments):
    moments[...] = jnp.zeros_like(moments)


def no_moments(width):
    return pl.pallas_call(
        no_moments_kernel,
        out_specs=pl.BlockSpec(memory_space=pltpu.VMEM),
        out_shape=jax.ShapeDtypeStruct((SUB, width), jnp.float32),
        compiler_params=pltpu.CompilerParams(vmem_limit_bytes=4 << 20),
        cost_estimate=pl.CostEstimate(
            flops=FIRST_EXCHANGE_FLOPS, bytes_accessed=4 * SUB * width, transcendentals=0
        ),
    )()


def leaving_rows(mig_rows, mig_count, blocks, width):
    capacity = mig_rows.shape[-1]
    live = lax.broadcasted_iota(jnp.int32, (2, capacity), 1) < mig_count[0, 0][:, None]
    rows = jnp.where(live, mig_rows[0, 0], -1).astype(jnp.float32)
    none = jnp.full((1, width - capacity), -1.0, jnp.float32)
    to_lower = jnp.concatenate([none, rows[0:1]], axis=1)
    to_upper = jnp.concatenate([rows[1:2], none], axis=1)
    rest = jnp.zeros((blocks - 2, width), jnp.float32)
    return jnp.concatenate([to_lower, to_upper, rest], axis=0)


def spread_sum(part, key):
    axial, cross = lax.axis_size("axial"), lax.axis_size("cross")
    groups = {}
    for a in range(axial):
        for c in range(cross):
            groups.setdefault(key(a, c), []).append(a * cross + c)
    groups = list(groups.values())
    if part.ndim == 2:
        part = jnp.broadcast_to(part[None], (len(groups[0]),) + part.shape)
    return lax.all_to_all(part, ("axial", "cross"), 0, 0, axis_index_groups=groups)


def on_device(force, self_drag, tiles, tile_ids, mig_rows, mig_count):
    field = jnp.swapaxes(force[0, 0], 0, 1)
    drag = self_drag[0, 0]
    blocks, width = drag.shape
    ids = tile_ids[0, 0]
    slab = lax.axis_index("cross")
    last = lax.axis_size("cross") - 1
    now, carried = field, (no_moments(width),)
    own, below, above, planes = [], [], [], []
    for sweep in range(ITERS):
        cross_dn = ring_shift(now, "cross", 1)
        cross_up = ring_shift(now, "cross", -1)
        axial_dn = ring_shift(now, "axial", 1)
        axial_up = ring_shift(now, "axial", -1)
        own.append(now)
        below.append(cross_dn)
        above.append(cross_up)
        r1, r3, r5, r7, kept, sums = operator_call(
            sweep, ids, (now, axial_dn, cross_dn, cross_up, axial_up), tiles[0, 0], drag, carried,
            2 * lax.axis_size("axial") if sweep == ITERS - 1 else None,
        )
        carried = (sums,)
        if sweep == ITERS - 1:
            part = jnp.sum(spread_sum(sums, lambda a, c: c // 2), axis=0)
            part, r1, r7 = lax.optimization_barrier((part, r1, r7))
        from_lower_cross = ring_shift(r5, "cross", 1)
        from_upper_cross = ring_shift(r3, "cross", -1)
        if sweep == ITERS - 1:
            part, from_lower_cross, from_upper_cross = lax.optimization_barrier(
                (part, from_lower_cross, from_upper_cross)
            )
            sums = spread_sum(part, lambda a, c: (a, c % 2))
        from_lower_axial = ring_shift(r7, "axial", 1)
        from_upper_axial = ring_shift(r1, "axial", -1)
        if sweep == 1:
            planes = [from_lower_cross, from_upper_cross]
        now = kept + from_lower_axial + from_upper_axial
        now = now + jnp.where(slab > 0, from_lower_cross[:3], 0.0)
        now = now + jnp.where(slab < last, from_upper_cross[:3], 0.0)
        if sweep == 0:
            now, mig_rows, mig_count = lax.optimization_barrier((now, mig_rows, mig_count))
            carried += (leaving_rows(mig_rows, mig_count, blocks, width),)
    own.append(now)
    velocity, residual, arrivals = finish_call(sums, own, below, above, planes)
    return (
        jnp.swapaxes(velocity, 0, 1)[None, None],
        jnp.swapaxes(residual, 0, 1)[None, None],
        jnp.swapaxes(arrivals, 0, 1)[None],
    )


def solution(mesh):
    placed = (
        P("axial", "cross", None, None, None),
        P("axial", "cross", None, None),
        P("axial", "cross", None, None, None, None),
        P("axial", "cross", None, None),
        P("axial", "cross", None, None),
        P("axial", "cross", None),
    )
    return jax.shard_map(
        on_device,
        mesh=mesh,
        in_specs=placed,
        out_specs=(
            P("axial", "cross", None, None, None),
            P("axial", "cross", None, None, None),
            P("axial", "cross", None, None),
        ),
        check_vma=False,
    )
```

```python
import functools

import jax
import jax.numpy as jnp
from jax import lax
from jax.experimental import pallas as pl
from jax.experimental.pallas import tpu as pltpu
from jax.sharding import PartitionSpec as P

ITERS = 3
PLACES = (1, 3, 4, 5, 7)
SUB = 8
FIRST_EXCHANGE_FLOPS = 8 * 10**9
LOW = 4


def ring(count, by):
    return [(i, (i + by) % count) for i in range(count)]


def ring_shift(shard, axis, by):
    return lax.ppermute(shard, axis, ring(lax.axis_size(axis), by))


def high_low(x):
    high = x.astype(jnp.bfloat16).astype(jnp.float32)
    return high, x - high


def operator_kernel(
    sweep, ids, own, from_axial_dn, from_cross_dn, from_cross_up, from_axial_up, tiles, drag, *rest
):
    many = 2 if sweep == ITERS - 1 else 1
    carried, rest = rest[:many], rest[many:]
    (
        to_axial_dn, to_cross_dn, to_cross_up, to_axial_up, kept, moments, ext, acc,
    ) = rest
    blocks, count = ids.shape
    width = tiles.shape[-1]
    slab = lax.axis_index("cross")
    has_dn = jnp.where(slab > 0, 1.0, 0.0).astype(jnp.float32)
    has_up = jnp.where(slab < lax.axis_size("cross") - 1, 1.0, 0.0).astype(jnp.float32)
    sources = (from_axial_dn, from_cross_dn, own, from_cross_up, from_axial_up)
    blank = jnp.zeros((blocks, width), jnp.float32)
    for place, source in zip(PLACES, sources):
        base = place * blocks * SUB
        for comp in range(3):
            x = source[comp]
            if place == 3:
                x = x * has_dn
            if place == 5:
                x = x * has_up
            high, low = high_low(x)
            ext[pl.ds(base + comp, blocks, stride=SUB), :] = high
            ext[pl.ds(base + LOW + comp, blocks, stride=SUB), :] = low
        ext[pl.ds(base + 3, blocks, stride=SUB), :] = blank
        ext[pl.ds(base + LOW + 3, blocks, stride=SUB), :] = blank
    acc[...] = jnp.zeros_like(acc)
    rows = lax.broadcasted_iota(jnp.int32, (SUB, width), 0)
    squares = jnp.zeros((SUB, width), jnp.float32)
    for b in range(blocks):
        starts = [pl.multiple_of(ids[b, k] * SUB, SUB) for k in range(count)]
        coupled = jnp.zeros((SUB, width), jnp.float32)
        for k in range(0, count, 2):
            picked = jnp.concatenate(
                [ext[pl.ds(starts[k], SUB), :], ext[pl.ds(starts[k + 1], SUB), :]], axis=1
            ).astype(jnp.bfloat16)
            pair = jnp.concatenate([tiles[b, k], tiles[b, k + 1]], axis=1)
            coupled += lax.dot_general(
                picked, pair, (((1,), (1,)), ((), ())), preferred_element_type=jnp.float32
            )
        coupled = coupled + pltpu.roll(coupled, LOW, 0)
        squares += jnp.where(rows < LOW, coupled * coupled, 0.0)
        high, low = high_low(coupled)
        parts = jnp.where(rows < LOW, high, low).astype(jnp.bfloat16)
        for k in range(count):
            acc[pl.ds(starts[k], SUB), :] += jnp.dot(
                parts, tiles[b, k], preferred_element_type=jnp.float32
            )
    targets = (to_axial_dn, to_cross_dn, None, to_cross_up, to_axial_up)
    even = jnp.zeros((blocks, width), jnp.float32)
    odd = squares
    for place, target in zip(PLACES, targets):
        base = place * blocks * SUB
        for comp in range(3):
            total = (
                acc[pl.ds(base + comp, blocks, stride=SUB), :]
                + acc[pl.ds(base + LOW + comp, blocks, stride=SUB), :]
            )
            if target is None:
                x = own[comp]
                dragged = drag[...] * x
                even += x * x
                odd += dragged * x
                kept[comp] = dragged + total
            else:
                target[comp] = total
    even = jnp.sum(even, axis=0, keepdims=True)
    odd = jnp.sum(odd, axis=0, keepdims=True)
    merged = jnp.where(
        rows == 2 * sweep, even, jnp.where(rows == 2 * sweep + 1, odd, carried[0][...])
    )
    moments[...] = jnp.broadcast_to(merged, moments.shape)
    if sweep == ITERS - 1:
        to_cross_dn[3] = carried[1][...]
        to_cross_up[3] = carried[1][...]


def operator_call(sweep, ids, sources, tiles, drag, carried, copies):
    blocks, width = drag.shape
    vmem = pl.BlockSpec(memory_space=pltpu.VMEM)
    field = jax.ShapeDtypeStruct((3, blocks, width), jnp.float32)
    across = jax.ShapeDtypeStruct((4 if sweep == ITERS - 1 else 3, blocks, width), jnp.float32)
    plane = (SUB, width) if copies is None else (copies, SUB, width)
    plane = jax.ShapeDtypeStruct(plane, jnp.float32)
    rows = 8 * blocks * SUB
    scratch = [pltpu.VMEM((rows, width), jnp.float32), pltpu.VMEM((rows, width), jnp.float32)]
    return pl.pallas_call(
        functools.partial(operator_kernel, sweep),
        in_specs=[pl.BlockSpec(memory_space=pltpu.SMEM)]
        + [vmem] * 5
        + [vmem] * (2 + len(carried)),
        out_specs=[vmem] * 6,
        out_shape=[field, across, across, field, field, plane],
        scratch_shapes=scratch,
        compiler_params=pltpu.CompilerParams(vmem_limit_bytes=4 << 20),
    )(ids, *sources, tiles, drag, *carried)


def shifted_poly(poly):
    return [None] + list(poly)


def combine(left, scale, right):
    out = []
    for i in range(max(len(left), len(right))):
        a = left[i] if i < len(left) else None
        b = right[i] if i < len(right) else None
        b = None if b is None else scale * b
        out.append(b if a is None else a if b is None else a + b)
    return out


def inner(left, right, shift, moment):
    total = None
    for i, a in enumerate(left):
        for j, b in enumerate(right):
            term = a * b * moment[i + j + shift]
            total = term if total is None else total + term
    return total


def cg_coefficients(moment):
    one = jnp.ones_like(moment[0])
    velocity, residual, direction = [], [one], [one]
    norm_now = moment[0]
    for sweep in range(ITERS):
        alpha = norm_now / inner(direction, direction, 1, moment)
        velocity = combine(velocity, alpha, direction)
        residual = combine(residual, -alpha, shifted_poly(direction))
        if sweep < ITERS - 1:
            norm_next = inner(residual, residual, 0, moment)
            direction = combine(residual, norm_next / norm_now, direction)
            norm_now = norm_next
    return velocity, residual


def mixed(coefs, fields):
    total = coefs[0] * fields[0]
    for c, f in zip(coefs[1:], fields[1:]):
        total = total + c * f
    return total


def picked_beads(fields, coefs, wanted, live):
    blocks, width = fields[0][0].shape
    index = jnp.where(live, wanted.astype(jnp.int32), -1)
    block = lax.shift_right_arithmetic(index, 7)
    place = jnp.bitwise_and(index, width - 1)
    parts = []
    for comp in range(3):
        x = mixed(coefs, [f[comp] for f in fields])
        high, rest = high_low(x)
        middle, low = high_low(rest)
        parts += [high, middle, low]
    stacked = jnp.concatenate(parts + [jnp.zeros_like(parts[0])], axis=0).astype(jnp.bfloat16)
    lanes = lax.broadcasted_iota(jnp.int32, (width, width), 0)
    chosen = jnp.where(lanes == place, 1.0, 0.0).astype(jnp.bfloat16)
    found = jnp.dot(stacked, chosen, preferred_element_type=jnp.float32)
    keep = lax.broadcasted_iota(jnp.int32, (blocks, width), 0) == block
    out = []
    for comp in range(3):
        at = 3 * comp * blocks
        x = (
            found[at : at + blocks]
            + found[at + blocks : at + 2 * blocks]
            + found[at + 2 * blocks : at + 3 * blocks]
        )
        out.append(jnp.sum(jnp.where(keep, x, 0.0), axis=0, keepdims=True))
    return out


def finish_kernel(
    sums, k0, k1, k2, k3, d0, d1, d2, u0, u1, u2, dn_plane, up_plane, velocity, residual, arrivals
):
    blocks, width = k0.shape[1:]
    slab = lax.axis_index("cross")
    total = jnp.sum(sums[...], axis=0)
    moment = [
        jnp.broadcast_to(jnp.sum(total[i : i + 1], axis=1, keepdims=True), (blocks, width))
        for i in range(2 * ITERS)
    ]
    vel, res = cg_coefficients(moment)
    own = (k0, k1, k2, k3)
    for comp in range(3):
        velocity[comp] = mixed(vel, [k[comp] for k in own[:ITERS]])
        residual[comp] = mixed(res, [k[comp] for k in own])
    lower = picked_beads((d0, d1, d2), vel, dn_plane[3, 1:2, :], slab > 0)
    upper = picked_beads(
        (u0, u1, u2), vel, up_plane[3, 0:1, :], slab < lax.axis_size("cross") - 1
    )
    for comp in range(3):
        arrivals[comp] = lower[comp] + upper[comp]


def finish_call(sums, own, below, above, planes):
    blocks, width = own[1].shape[1:]
    vmem = pl.BlockSpec(memory_space=pltpu.VMEM)
    field = jax.ShapeDtypeStruct((3, blocks, width), jnp.float32)
    return pl.pallas_call(
        finish_kernel,
        in_specs=[vmem] * 13,
        out_specs=[vmem] * 3,
        out_shape=[field, field, jax.ShapeDtypeStruct((3, 1, width), jnp.float32)],
        compiler_params=pltpu.CompilerParams(vmem_limit_bytes=4 << 20),
    )(sums, *own, *below, *above, *planes)


def no_moments_kernel(moments):
    moments[...] = jnp.zeros_like(moments)


def no_moments(width):
    return pl.pallas_call(
        no_moments_kernel,
        out_specs=pl.BlockSpec(memory_space=pltpu.VMEM),
        out_shape=jax.ShapeDtypeStruct((SUB, width), jnp.float32),
        compiler_params=pltpu.CompilerParams(vmem_limit_bytes=4 << 20),
        cost_estimate=pl.CostEstimate(
            flops=FIRST_EXCHANGE_FLOPS, bytes_accessed=4 * SUB * width, transcendentals=0
        ),
    )()


def leaving_rows(mig_rows, mig_count, blocks, width):
    capacity = mig_rows.shape[-1]
    live = lax.broadcasted_iota(jnp.int32, (2, capacity), 1) < mig_count[0, 0][:, None]
    rows = jnp.where(live, mig_rows[0, 0], -1).astype(jnp.float32)
    none = jnp.full((1, width - capacity), -1.0, jnp.float32)
    to_lower = jnp.concatenate([none, rows[0:1]], axis=1)
    to_upper = jnp.concatenate([rows[1:2], none], axis=1)
    rest = jnp.zeros((blocks - 2, width), jnp.float32)
    return jnp.concatenate([to_lower, to_upper, rest], axis=0)


def spread_sum(part, key):
    axial, cross = lax.axis_size("axial"), lax.axis_size("cross")
    groups = {}
    for a in range(axial):
        for c in range(cross):
            groups.setdefault(key(a, c), []).append(a * cross + c)
    groups = list(groups.values())
    if part.ndim == 2:
        part = jnp.broadcast_to(part[None], (len(groups[0]),) + part.shape)
    return lax.all_to_all(part, ("axial", "cross"), 0, 0, axis_index_groups=groups)


def on_device(force, self_drag, tiles, tile_ids, mig_rows, mig_count):
    field = jnp.swapaxes(force[0, 0], 0, 1)
    drag = self_drag[0, 0]
    blocks, width = drag.shape
    ids = tile_ids[0, 0]
    slab = lax.axis_index("cross")
    last = lax.axis_size("cross") - 1
    now, carried = field, (no_moments(width),)
    own, below, above, planes = [], [], [], []
    for sweep in range(ITERS):
        cross_dn = ring_shift(now, "cross", 1)
        cross_up = ring_shift(now, "cross", -1)
        axial_dn = ring_shift(now, "axial", 1)
        axial_up = ring_shift(now, "axial", -1)
        own.append(now)
        below.append(cross_dn)
        above.append(cross_up)
        r1, r3, r5, r7, kept, sums = operator_call(
            sweep, ids, (now, axial_dn, cross_dn, cross_up, axial_up), tiles[0, 0], drag, carried,
            2 * lax.axis_size("axial") if sweep == ITERS - 1 else None,
        )
        carried = (sums,)
        if sweep == ITERS - 1:
            part = jnp.sum(spread_sum(sums, lambda a, c: c // 2), axis=0)
            part, r1, r7 = lax.optimization_barrier((part, r1, r7))
        from_lower_cross = ring_shift(r5, "cross", 1)
        from_upper_cross = ring_shift(r3, "cross", -1)
        if sweep == ITERS - 1:
            part, from_lower_cross, from_upper_cross = lax.optimization_barrier(
                (part, from_lower_cross, from_upper_cross)
            )
            sums = spread_sum(part, lambda a, c: (a, c % 2))
        from_lower_axial = ring_shift(r7, "axial", 1)
        from_upper_axial = ring_shift(r1, "axial", -1)
        if sweep == ITERS - 1:
            planes = [from_lower_cross, from_upper_cross]
        now = kept + from_lower_axial + from_upper_axial
        now = now + jnp.where(slab > 0, from_lower_cross[:3], 0.0)
        now = now + jnp.where(slab < last, from_upper_cross[:3], 0.0)
        if sweep == ITERS - 2:
            now, mig_rows, mig_count = lax.optimization_barrier((now, mig_rows, mig_count))
            carried += (leaving_rows(mig_rows, mig_count, blocks, width),)
    own.append(now)
    velocity, residual, arrivals = finish_call(sums, own, below, above, planes)
    return (
        jnp.swapaxes(velocity, 0, 1)[None, None],
        jnp.swapaxes(residual, 0, 1)[None, None],
        jnp.swapaxes(arrivals, 0, 1)[None],
    )


def solution(mesh):
    placed = (
        P("axial", "cross", None, None, None),
        P("axial", "cross", None, None),
        P("axial", "cross", None, None, None, None),
        P("axial", "cross", None, None),
        P("axial", "cross", None, None),
        P("axial", "cross", None),
    )
    return jax.shard_map(
        on_device,
        mesh=mesh,
        in_specs=placed,
        out_specs=(
            P("axial", "cross", None, None, None),
            P("axial", "cross", None, None, None),
            P("axial", "cross", None, None),
        ),
        check_vma=False,
    )
```

```python
import functools

import jax
import jax.numpy as jnp
from jax import lax
from jax.experimental import pallas as pl
from jax.experimental.pallas import tpu as pltpu
from jax.sharding import PartitionSpec as P

ITERS = 3
PLACES = (1, 3, 4, 5, 7)
SUB = 8
FIRST_EXCHANGE_FLOPS = 8 * 10**9
LOW = 4


def ring(count, by):
    return [(i, (i + by) % count) for i in range(count)]


def ring_shift(shard, axis, by):
    return lax.ppermute(shard, axis, ring(lax.axis_size(axis), by))


def high_low(x):
    high = x.astype(jnp.bfloat16).astype(jnp.float32)
    return high, x - high


def operator_kernel(
    sweep, ids, own, from_cross_up, from_cross_dn, from_axial_up, from_axial_dn, tiles, drag, *rest
):
    many = 2 if sweep == ITERS - 1 else 1
    carried, rest = rest[:many], rest[many:]
    (
        to_axial_dn, to_cross_dn, to_cross_up, to_axial_up, kept, moments, ext, acc,
    ) = rest
    blocks, count = ids.shape
    width = tiles.shape[-1]
    slab = lax.axis_index("cross")
    has_dn = jnp.where(slab > 0, 1.0, 0.0).astype(jnp.float32)
    has_up = jnp.where(slab < lax.axis_size("cross") - 1, 1.0, 0.0).astype(jnp.float32)
    sources = (from_axial_dn, from_cross_dn, own, from_cross_up, from_axial_up)
    blank = jnp.zeros((blocks, width), jnp.float32)
    for place, source in zip(PLACES, sources):
        base = place * blocks * SUB
        for comp in range(3):
            x = source[comp]
            if place == 3:
                x = x * has_dn
            if place == 5:
                x = x * has_up
            high, low = high_low(x)
            ext[pl.ds(base + comp, blocks, stride=SUB), :] = high
            ext[pl.ds(base + LOW + comp, blocks, stride=SUB), :] = low
        ext[pl.ds(base + 3, blocks, stride=SUB), :] = blank
        ext[pl.ds(base + LOW + 3, blocks, stride=SUB), :] = blank
    acc[...] = jnp.zeros_like(acc)
    rows = lax.broadcasted_iota(jnp.int32, (SUB, width), 0)
    squares = jnp.zeros((SUB, width), jnp.float32)
    for b in range(blocks):
        starts = [pl.multiple_of(ids[b, k] * SUB, SUB) for k in range(count)]
        coupled = jnp.zeros((SUB, width), jnp.float32)
        for k in range(0, count, 2):
            picked = jnp.concatenate(
                [ext[pl.ds(starts[k], SUB), :], ext[pl.ds(starts[k + 1], SUB), :]], axis=1
            ).astype(jnp.bfloat16)
            pair = jnp.concatenate([tiles[b, k], tiles[b, k + 1]], axis=1)
            coupled += lax.dot_general(
                picked, pair, (((1,), (1,)), ((), ())), preferred_element_type=jnp.float32
            )
        coupled = coupled + pltpu.roll(coupled, LOW, 0)
        squares += jnp.where(rows < LOW, coupled * coupled, 0.0)
        high, low = high_low(coupled)
        parts = jnp.where(rows < LOW, high, low).astype(jnp.bfloat16)
        for k in range(count):
            acc[pl.ds(starts[k], SUB), :] += jnp.dot(
                parts, tiles[b, k], preferred_element_type=jnp.float32
            )
    targets = (to_axial_dn, to_cross_dn, None, to_cross_up, to_axial_up)
    even = jnp.zeros((blocks, width), jnp.float32)
    odd = squares
    for place, target in zip(PLACES, targets):
        base = place * blocks * SUB
        for comp in range(3):
            total = (
                acc[pl.ds(base + comp, blocks, stride=SUB), :]
                + acc[pl.ds(base + LOW + comp, blocks, stride=SUB), :]
            )
            if target is None:
                x = own[comp]
                dragged = drag[...] * x
                even += x * x
                odd += dragged * x
                kept[comp] = dragged + total
            else:
                target[comp] = total
    even = jnp.sum(even, axis=0, keepdims=True)
    odd = jnp.sum(odd, axis=0, keepdims=True)
    merged = jnp.where(
        rows == 2 * sweep, even, jnp.where(rows == 2 * sweep + 1, odd, carried[0][...])
    )
    moments[...] = jnp.broadcast_to(merged, moments.shape)
    if sweep == ITERS - 1:
        to_cross_dn[3] = carried[1][...]
        to_cross_up[3] = carried[1][...]


def operator_call(sweep, ids, sources, tiles, drag, carried, copies):
    blocks, width = drag.shape
    vmem = pl.BlockSpec(memory_space=pltpu.VMEM)
    field = jax.ShapeDtypeStruct((3, blocks, width), jnp.float32)
    across = jax.ShapeDtypeStruct((4 if sweep == ITERS - 1 else 3, blocks, width), jnp.float32)
    plane = (SUB, width) if copies is None else (copies, SUB, width)
    plane = jax.ShapeDtypeStruct(plane, jnp.float32)
    rows = 8 * blocks * SUB
    scratch = [pltpu.VMEM((rows, width), jnp.float32), pltpu.VMEM((rows, width), jnp.float32)]
    return pl.pallas_call(
        functools.partial(operator_kernel, sweep),
        in_specs=[pl.BlockSpec(memory_space=pltpu.SMEM)]
        + [vmem] * 5
        + [vmem] * (2 + len(carried)),
        out_specs=[vmem] * 6,
        out_shape=[field, across, across, field, field, plane],
        scratch_shapes=scratch,
        compiler_params=pltpu.CompilerParams(vmem_limit_bytes=4 << 20),
    )(ids, *sources, tiles, drag, *carried)


def shifted_poly(poly):
    return [None] + list(poly)


def combine(left, scale, right):
    out = []
    for i in range(max(len(left), len(right))):
        a = left[i] if i < len(left) else None
        b = right[i] if i < len(right) else None
        b = None if b is None else scale * b
        out.append(b if a is None else a if b is None else a + b)
    return out


def inner(left, right, shift, moment):
    total = None
    for i, a in enumerate(left):
        for j, b in enumerate(right):
            term = a * b * moment[i + j + shift]
            total = term if total is None else total + term
    return total


def cg_coefficients(moment):
    one = jnp.ones_like(moment[0])
    velocity, residual, direction = [], [one], [one]
    norm_now = moment[0]
    for sweep in range(ITERS):
        alpha = norm_now / inner(direction, direction, 1, moment)
        velocity = combine(velocity, alpha, direction)
        residual = combine(residual, -alpha, shifted_poly(direction))
        if sweep < ITERS - 1:
            norm_next = inner(residual, residual, 0, moment)
            direction = combine(residual, norm_next / norm_now, direction)
            norm_now = norm_next
    return velocity, residual


def mixed(coefs, fields):
    total = coefs[0] * fields[0]
    for c, f in zip(coefs[1:], fields[1:]):
        total = total + c * f
    return total


def picked_beads(fields, coefs, wanted, live):
    blocks, width = fields[0][0].shape
    index = jnp.where(live, wanted.astype(jnp.int32), -1)
    block = lax.shift_right_arithmetic(index, 7)
    place = jnp.bitwise_and(index, width - 1)
    parts = []
    for comp in range(3):
        x = mixed(coefs, [f[comp] for f in fields])
        high, rest = high_low(x)
        middle, low = high_low(rest)
        parts += [high, middle, low]
    stacked = jnp.concatenate(parts + [jnp.zeros_like(parts[0])], axis=0).astype(jnp.bfloat16)
    lanes = lax.broadcasted_iota(jnp.int32, (width, width), 0)
    chosen = jnp.where(lanes == place, 1.0, 0.0).astype(jnp.bfloat16)
    found = jnp.dot(stacked, chosen, preferred_element_type=jnp.float32)
    keep = lax.broadcasted_iota(jnp.int32, (blocks, width), 0) == block
    out = []
    for comp in range(3):
        at = 3 * comp * blocks
        x = (
            found[at : at + blocks]
            + found[at + blocks : at + 2 * blocks]
            + found[at + 2 * blocks : at + 3 * blocks]
        )
        out.append(jnp.sum(jnp.where(keep, x, 0.0), axis=0, keepdims=True))
    return out


def finish_kernel(
    sums, k0, k1, k2, k3, d0, d1, d2, u0, u1, u2, dn_plane, up_plane, velocity, residual, arrivals
):
    blocks, width = k0.shape[1:]
    slab = lax.axis_index("cross")
    total = jnp.sum(sums[...], axis=0)
    moment = [
        jnp.broadcast_to(jnp.sum(total[i : i + 1], axis=1, keepdims=True), (blocks, width))
        for i in range(2 * ITERS)
    ]
    vel, res = cg_coefficients(moment)
    own = (k0, k1, k2, k3)
    for comp in range(3):
        velocity[comp] = mixed(vel, [k[comp] for k in own[:ITERS]])
        residual[comp] = mixed(res, [k[comp] for k in own])
    lower = picked_beads((d0, d1, d2), vel, dn_plane[3, 1:2, :], slab > 0)
    upper = picked_beads(
        (u0, u1, u2), vel, up_plane[3, 0:1, :], slab < lax.axis_size("cross") - 1
    )
    for comp in range(3):
        arrivals[comp] = lower[comp] + upper[comp]


def finish_call(sums, own, below, above, planes):
    blocks, width = own[1].shape[1:]
    vmem = pl.BlockSpec(memory_space=pltpu.VMEM)
    field = jax.ShapeDtypeStruct((3, blocks, width), jnp.float32)
    return pl.pallas_call(
        finish_kernel,
        in_specs=[vmem] * 13,
        out_specs=[vmem] * 3,
        out_shape=[field, field, jax.ShapeDtypeStruct((3, 1, width), jnp.float32)],
        compiler_params=pltpu.CompilerParams(vmem_limit_bytes=4 << 20),
    )(sums, *own, *below, *above, *planes)


def no_moments_kernel(moments):
    moments[...] = jnp.zeros_like(moments)


def no_moments(width):
    return pl.pallas_call(
        no_moments_kernel,
        out_specs=pl.BlockSpec(memory_space=pltpu.VMEM),
        out_shape=jax.ShapeDtypeStruct((SUB, width), jnp.float32),
        compiler_params=pltpu.CompilerParams(vmem_limit_bytes=4 << 20),
        cost_estimate=pl.CostEstimate(
            flops=FIRST_EXCHANGE_FLOPS, bytes_accessed=4 * SUB * width, transcendentals=0
        ),
    )()


def leaving_rows(mig_rows, mig_count, blocks, width):
    capacity = mig_rows.shape[-1]
    live = lax.broadcasted_iota(jnp.int32, (2, capacity), 1) < mig_count[0, 0][:, None]
    rows = jnp.where(live, mig_rows[0, 0], -1).astype(jnp.float32)
    none = jnp.full((1, width - capacity), -1.0, jnp.float32)
    to_lower = jnp.concatenate([none, rows[0:1]], axis=1)
    to_upper = jnp.concatenate([rows[1:2], none], axis=1)
    rest = jnp.zeros((blocks - 2, width), jnp.float32)
    return jnp.concatenate([to_lower, to_upper, rest], axis=0)


def spread_sum(part, key):
    axial, cross = lax.axis_size("axial"), lax.axis_size("cross")
    groups = {}
    for a in range(axial):
        for c in range(cross):
            groups.setdefault(key(a, c), []).append(a * cross + c)
    groups = list(groups.values())
    if part.ndim == 2:
        part = jnp.broadcast_to(part[None], (len(groups[0]),) + part.shape)
    return lax.all_to_all(part, ("axial", "cross"), 0, 0, axis_index_groups=groups)


def on_device(force, self_drag, tiles, tile_ids, mig_rows, mig_count):
    field = jnp.swapaxes(force[0, 0], 0, 1)
    drag = self_drag[0, 0]
    blocks, width = drag.shape
    ids = tile_ids[0, 0]
    slab = lax.axis_index("cross")
    last = lax.axis_size("cross") - 1
    now, carried = field, (no_moments(width),)
    own, below, above, planes = [], [], [], []
    for sweep in range(ITERS):
        cross_dn = ring_shift(now, "cross", 1)
        cross_up = ring_shift(now, "cross", -1)
        axial_dn = ring_shift(now, "axial", 1)
        axial_up = ring_shift(now, "axial", -1)
        own.append(now)
        below.append(cross_dn)
        above.append(cross_up)
        r1, r3, r5, r7, kept, sums = operator_call(
            sweep, ids, (now, cross_up, cross_dn, axial_up, axial_dn), tiles[0, 0], drag, carried,
            2 * lax.axis_size("axial") if sweep == ITERS - 1 else None,
        )
        carried = (sums,)
        if sweep == ITERS - 1:
            part = jnp.sum(spread_sum(sums, lambda a, c: c // 2), axis=0)
            part, r1, r7 = lax.optimization_barrier((part, r1, r7))
        from_lower_cross = ring_shift(r5, "cross", 1)
        from_upper_cross = ring_shift(r3, "cross", -1)
        if sweep == ITERS - 1:
            part, from_lower_cross, from_upper_cross = lax.optimization_barrier(
                (part, from_lower_cross, from_upper_cross)
            )
            sums = spread_sum(part, lambda a, c: (a, c % 2))
        from_lower_axial = ring_shift(r7, "axial", 1)
        from_upper_axial = ring_shift(r1, "axial", -1)
        if sweep == ITERS - 1:
            planes = [from_lower_cross, from_upper_cross]
        now = kept + from_lower_axial + from_upper_axial
        now = now + jnp.where(slab > 0, from_lower_cross[:3], 0.0)
        now = now + jnp.where(slab < last, from_upper_cross[:3], 0.0)
        if sweep == ITERS - 2:
            now, mig_rows, mig_count = lax.optimization_barrier((now, mig_rows, mig_count))
            carried += (leaving_rows(mig_rows, mig_count, blocks, width),)
    own.append(now)
    velocity, residual, arrivals = finish_call(sums, own, below, above, planes)
    return (
        jnp.swapaxes(velocity, 0, 1)[None, None],
        jnp.swapaxes(residual, 0, 1)[None, None],
        jnp.swapaxes(arrivals, 0, 1)[None],
    )


def solution(mesh):
    placed = (
        P("axial", "cross", None, None, None),
        P("axial", "cross", None, None),
        P("axial", "cross", None, None, None, None),
        P("axial", "cross", None, None),
        P("axial", "cross", None, None),
        P("axial", "cross", None),
    )
    return jax.shard_map(
        on_device,
        mesh=mesh,
        in_specs=placed,
        out_specs=(
            P("axial", "cross", None, None, None),
            P("axial", "cross", None, None, None),
            P("axial", "cross", None, None),
        ),
        check_vma=False,
    )
```

```python
import functools

import jax
import jax.numpy as jnp
from jax import lax
from jax.experimental import pallas as pl
from jax.experimental.pallas import tpu as pltpu
from jax.sharding import PartitionSpec as P

ITERS = 3
PLACES = (1, 3, 4, 5, 7)
SUB = 8
FIRST_EXCHANGE_FLOPS = 8 * 10**9
LOW = 4


def ring(count, by):
    return [(i, (i + by) % count) for i in range(count)]


def ring_shift(shard, axis, by):
    return lax.ppermute(shard, axis, ring(lax.axis_size(axis), by))


def high_low(x):
    high = x.astype(jnp.bfloat16).astype(jnp.float32)
    return high, x - high


def operator_kernel(
    sweep, ids, own, from_cross_up, from_axial_up, from_cross_dn, from_axial_dn, tiles, drag, *rest
):
    many = 2 if sweep == ITERS - 1 else 1
    carried, rest = rest[:many], rest[many:]
    (
        to_axial_dn, to_cross_dn, to_cross_up, to_axial_up, kept, moments, ext, acc,
    ) = rest
    blocks, count = ids.shape
    width = tiles.shape[-1]
    slab = lax.axis_index("cross")
    has_dn = jnp.where(slab > 0, 1.0, 0.0).astype(jnp.float32)
    has_up = jnp.where(slab < lax.axis_size("cross") - 1, 1.0, 0.0).astype(jnp.float32)
    sources = (from_axial_dn, from_cross_dn, own, from_cross_up, from_axial_up)
    blank = jnp.zeros((blocks, width), jnp.float32)
    for place, source in zip(PLACES, sources):
        base = place * blocks * SUB
        for comp in range(3):
            x = source[comp]
            if place == 3:
                x = x * has_dn
            if place == 5:
                x = x * has_up
            high, low = high_low(x)
            ext[pl.ds(base + comp, blocks, stride=SUB), :] = high
            ext[pl.ds(base + LOW + comp, blocks, stride=SUB), :] = low
        ext[pl.ds(base + 3, blocks, stride=SUB), :] = blank
        ext[pl.ds(base + LOW + 3, blocks, stride=SUB), :] = blank
    acc[...] = jnp.zeros_like(acc)
    rows = lax.broadcasted_iota(jnp.int32, (SUB, width), 0)
    squares = jnp.zeros((SUB, width), jnp.float32)
    for b in range(blocks):
        starts = [pl.multiple_of(ids[b, k] * SUB, SUB) for k in range(count)]
        coupled = jnp.zeros((SUB, width), jnp.float32)
        for k in range(0, count, 2):
            picked = jnp.concatenate(
                [ext[pl.ds(starts[k], SUB), :], ext[pl.ds(starts[k + 1], SUB), :]], axis=1
            ).astype(jnp.bfloat16)
            pair = jnp.concatenate([tiles[b, k], tiles[b, k + 1]], axis=1)
            coupled += lax.dot_general(
                picked, pair, (((1,), (1,)), ((), ())), preferred_element_type=jnp.float32
            )
        coupled = coupled + pltpu.roll(coupled, LOW, 0)
        squares += jnp.where(rows < LOW, coupled * coupled, 0.0)
        high, low = high_low(coupled)
        parts = jnp.where(rows < LOW, high, low).astype(jnp.bfloat16)
        for k in range(count):
            acc[pl.ds(starts[k], SUB), :] += jnp.dot(
                parts, tiles[b, k], preferred_element_type=jnp.float32
            )
    targets = (to_axial_dn, to_cross_dn, None, to_cross_up, to_axial_up)
    even = jnp.zeros((blocks, width), jnp.float32)
    odd = squares
    for place, target in zip(PLACES, targets):
        base = place * blocks * SUB
        for comp in range(3):
            total = (
                acc[pl.ds(base + comp, blocks, stride=SUB), :]
                + acc[pl.ds(base + LOW + comp, blocks, stride=SUB), :]
            )
            if target is None:
                x = own[comp]
                dragged = drag[...] * x
                even += x * x
                odd += dragged * x
                kept[comp] = dragged + total
            else:
                target[comp] = total
    even = jnp.sum(even, axis=0, keepdims=True)
    odd = jnp.sum(odd, axis=0, keepdims=True)
    merged = jnp.where(
        rows == 2 * sweep, even, jnp.where(rows == 2 * sweep + 1, odd, carried[0][...])
    )
    moments[...] = jnp.broadcast_to(merged, moments.shape)
    if sweep == ITERS - 1:
        to_cross_dn[3] = carried[1][...]
        to_cross_up[3] = carried[1][...]


def operator_call(sweep, ids, sources, tiles, drag, carried, copies):
    blocks, width = drag.shape
    vmem = pl.BlockSpec(memory_space=pltpu.VMEM)
    field = jax.ShapeDtypeStruct((3, blocks, width), jnp.float32)
    across = jax.ShapeDtypeStruct((4 if sweep == ITERS - 1 else 3, blocks, width), jnp.float32)
    plane = (SUB, width) if copies is None else (copies, SUB, width)
    plane = jax.ShapeDtypeStruct(plane, jnp.float32)
    rows = 8 * blocks * SUB
    scratch = [pltpu.VMEM((rows, width), jnp.float32), pltpu.VMEM((rows, width), jnp.float32)]
    return pl.pallas_call(
        functools.partial(operator_kernel, sweep),
        in_specs=[pl.BlockSpec(memory_space=pltpu.SMEM)]
        + [vmem] * 5
        + [vmem] * (2 + len(carried)),
        out_specs=[vmem] * 6,
        out_shape=[field, across, across, field, field, plane],
        scratch_shapes=scratch,
        compiler_params=pltpu.CompilerParams(vmem_limit_bytes=4 << 20),
    )(ids, *sources, tiles, drag, *carried)


def shifted_poly(poly):
    return [None] + list(poly)


def combine(left, scale, right):
    out = []
    for i in range(max(len(left), len(right))):
        a = left[i] if i < len(left) else None
        b = right[i] if i < len(right) else None
        b = None if b is None else scale * b
        out.append(b if a is None else a if b is None else a + b)
    return out


def inner(left, right, shift, moment):
    total = None
    for i, a in enumerate(left):
        for j, b in enumerate(right):
            term = a * b * moment[i + j + shift]
            total = term if total is None else total + term
    return total


def cg_coefficients(moment):
    one = jnp.ones_like(moment[0])
    velocity, residual, direction = [], [one], [one]
    norm_now = moment[0]
    for sweep in range(ITERS):
        alpha = norm_now / inner(direction, direction, 1, moment)
        velocity = combine(velocity, alpha, direction)
        residual = combine(residual, -alpha, shifted_poly(direction))
        if sweep < ITERS - 1:
            norm_next = inner(residual, residual, 0, moment)
            direction = combine(residual, norm_next / norm_now, direction)
            norm_now = norm_next
    return velocity, residual


def mixed(coefs, fields):
    total = coefs[0] * fields[0]
    for c, f in zip(coefs[1:], fields[1:]):
        total = total + c * f
    return total


def picked_beads(fields, coefs, wanted, live):
    blocks, width = fields[0][0].shape
    index = jnp.where(live, wanted.astype(jnp.int32), -1)
    block = lax.shift_right_arithmetic(index, 7)
    place = jnp.bitwise_and(index, width - 1)
    parts = []
    for comp in range(3):
        x = mixed(coefs, [f[comp] for f in fields])
        high, rest = high_low(x)
        middle, low = high_low(rest)
        parts += [high, middle, low]
    stacked = jnp.concatenate(parts + [jnp.zeros_like(parts[0])], axis=0).astype(jnp.bfloat16)
    lanes = lax.broadcasted_iota(jnp.int32, (width, width), 0)
    chosen = jnp.where(lanes == place, 1.0, 0.0).astype(jnp.bfloat16)
    found = jnp.dot(stacked, chosen, preferred_element_type=jnp.float32)
    keep = lax.broadcasted_iota(jnp.int32, (blocks, width), 0) == block
    out = []
    for comp in range(3):
        at = 3 * comp * blocks
        x = (
            found[at : at + blocks]
            + found[at + blocks : at + 2 * blocks]
            + found[at + 2 * blocks : at + 3 * blocks]
        )
        out.append(jnp.sum(jnp.where(keep, x, 0.0), axis=0, keepdims=True))
    return out


def finish_kernel(
    sums, k0, k1, k2, k3, d0, d1, d2, u0, u1, u2, dn_plane, up_plane, velocity, residual, arrivals
):
    blocks, width = k0.shape[1:]
    slab = lax.axis_index("cross")
    total = jnp.sum(sums[...], axis=0)
    moment = [
        jnp.broadcast_to(jnp.sum(total[i : i + 1], axis=1, keepdims=True), (blocks, width))
        for i in range(2 * ITERS)
    ]
    vel, res = cg_coefficients(moment)
    own = (k0, k1, k2, k3)
    for comp in range(3):
        velocity[comp] = mixed(vel, [k[comp] for k in own[:ITERS]])
        residual[comp] = mixed(res, [k[comp] for k in own])
    lower = picked_beads((d0, d1, d2), vel, dn_plane[3, 1:2, :], slab > 0)
    upper = picked_beads(
        (u0, u1, u2), vel, up_plane[3, 0:1, :], slab < lax.axis_size("cross") - 1
    )
    for comp in range(3):
        arrivals[comp] = lower[comp] + upper[comp]


def finish_call(sums, own, below, above, planes):
    blocks, width = own[1].shape[1:]
    vmem = pl.BlockSpec(memory_space=pltpu.VMEM)
    field = jax.ShapeDtypeStruct((3, blocks, width), jnp.float32)
    return pl.pallas_call(
        finish_kernel,
        in_specs=[vmem] * 13,
        out_specs=[vmem] * 3,
        out_shape=[field, field, jax.ShapeDtypeStruct((3, 1, width), jnp.float32)],
        compiler_params=pltpu.CompilerParams(vmem_limit_bytes=4 << 20),
    )(sums, *own, *below, *above, *planes)


def no_moments_kernel(moments):
    moments[...] = jnp.zeros_like(moments)


def no_moments(width):
    return pl.pallas_call(
        no_moments_kernel,
        out_specs=pl.BlockSpec(memory_space=pltpu.VMEM),
        out_shape=jax.ShapeDtypeStruct((SUB, width), jnp.float32),
        compiler_params=pltpu.CompilerParams(vmem_limit_bytes=4 << 20),
        cost_estimate=pl.CostEstimate(
            flops=FIRST_EXCHANGE_FLOPS, bytes_accessed=4 * SUB * width, transcendentals=0
        ),
    )()


def leaving_rows(mig_rows, mig_count, blocks, width):
    capacity = mig_rows.shape[-1]
    live = lax.broadcasted_iota(jnp.int32, (2, capacity), 1) < mig_count[0, 0][:, None]
    rows = jnp.where(live, mig_rows[0, 0], -1).astype(jnp.float32)
    none = jnp.full((1, width - capacity), -1.0, jnp.float32)
    to_lower = jnp.concatenate([none, rows[0:1]], axis=1)
    to_upper = jnp.concatenate([rows[1:2], none], axis=1)
    rest = jnp.zeros((blocks - 2, width), jnp.float32)
    return jnp.concatenate([to_lower, to_upper, rest], axis=0)


def spread_sum(part, key):
    axial, cross = lax.axis_size("axial"), lax.axis_size("cross")
    groups = {}
    for a in range(axial):
        for c in range(cross):
            groups.setdefault(key(a, c), []).append(a * cross + c)
    groups = list(groups.values())
    if part.ndim == 2:
        part = jnp.broadcast_to(part[None], (len(groups[0]),) + part.shape)
    return lax.all_to_all(part, ("axial", "cross"), 0, 0, axis_index_groups=groups)


def on_device(force, self_drag, tiles, tile_ids, mig_rows, mig_count):
    field = jnp.swapaxes(force[0, 0], 0, 1)
    drag = self_drag[0, 0]
    blocks, width = drag.shape
    ids = tile_ids[0, 0]
    slab = lax.axis_index("cross")
    last = lax.axis_size("cross") - 1
    now, carried = field, (no_moments(width),)
    own, below, above, planes = [], [], [], []
    for sweep in range(ITERS):
        cross_dn = ring_shift(now, "cross", 1)
        cross_up = ring_shift(now, "cross", -1)
        axial_dn = ring_shift(now, "axial", 1)
        axial_up = ring_shift(now, "axial", -1)
        own.append(now)
        below.append(cross_dn)
        above.append(cross_up)
        r1, r3, r5, r7, kept, sums = operator_call(
            sweep, ids, (now, cross_up, axial_up, cross_dn, axial_dn), tiles[0, 0], drag, carried,
            2 * lax.axis_size("axial") if sweep == ITERS - 1 else None,
        )
        carried = (sums,)
        if sweep == ITERS - 1:
            part = jnp.sum(spread_sum(sums, lambda a, c: c // 2), axis=0)
            part, r1, r7 = lax.optimization_barrier((part, r1, r7))
        from_lower_cross = ring_shift(r5, "cross", 1)
        from_upper_cross = ring_shift(r3, "cross", -1)
        if sweep == ITERS - 1:
            part, from_lower_cross, from_upper_cross = lax.optimization_barrier(
                (part, from_lower_cross, from_upper_cross)
            )
            sums = spread_sum(part, lambda a, c: (a, c % 2))
        from_lower_axial = ring_shift(r7, "axial", 1)
        from_upper_axial = ring_shift(r1, "axial", -1)
        if sweep == ITERS - 1:
            planes = [from_lower_cross, from_upper_cross]
        now = kept + from_lower_axial
        now = now + jnp.where(slab > 0, from_lower_cross[:3], 0.0)
        now = now + from_upper_axial
        now = now + jnp.where(slab < last, from_upper_cross[:3], 0.0)
        if sweep == ITERS - 2:
            now, mig_rows, mig_count = lax.optimization_barrier((now, mig_rows, mig_count))
            carried += (leaving_rows(mig_rows, mig_count, blocks, width),)
    own.append(now)
    velocity, residual, arrivals = finish_call(sums, own, below, above, planes)
    return (
        jnp.swapaxes(velocity, 0, 1)[None, None],
        jnp.swapaxes(residual, 0, 1)[None, None],
        jnp.swapaxes(arrivals, 0, 1)[None],
    )


def solution(mesh):
    placed = (
        P("axial", "cross", None, None, None),
        P("axial", "cross", None, None),
        P("axial", "cross", None, None, None, None),
        P("axial", "cross", None, None),
        P("axial", "cross", None, None),
        P("axial", "cross", None),
    )
    return jax.shard_map(
        on_device,
        mesh=mesh,
        in_specs=placed,
        out_specs=(
            P("axial", "cross", None, None, None),
            P("axial", "cross", None, None, None),
            P("axial", "cross", None, None),
        ),
        check_vma=False,
    )
```

```python
import functools

import jax
import jax.numpy as jnp
from jax import lax
from jax.experimental import pallas as pl
from jax.experimental.pallas import tpu as pltpu
from jax.sharding import PartitionSpec as P

ITERS = 3
PLACES = (1, 3, 4, 5, 7)
SUB = 8
FIRST_EXCHANGE_FLOPS = 8 * 10**9
LOW = 4


def ring(count, by):
    return [(i, (i + by) % count) for i in range(count)]


def ring_shift(shard, axis, by):
    return lax.ppermute(shard, axis, ring(lax.axis_size(axis), by))


def high_low(x):
    high = x.astype(jnp.bfloat16).astype(jnp.float32)
    return high, x - high


def operator_kernel(
    sweep, ids, own, from_cross_up, from_axial_up, from_cross_dn, from_axial_dn, tiles, drag, *rest
):
    many = 2 if sweep == ITERS - 1 else 1
    carried, rest = rest[:many], rest[many:]
    (
        to_axial_dn, to_cross_dn, to_cross_up, to_axial_up, kept, moments, ext, acc,
    ) = rest
    blocks, count = ids.shape
    width = tiles.shape[-1]
    slab = lax.axis_index("cross")
    has_dn = jnp.where(slab > 0, 1.0, 0.0).astype(jnp.float32)
    has_up = jnp.where(slab < lax.axis_size("cross") - 1, 1.0, 0.0).astype(jnp.float32)
    sources = (from_axial_dn, from_cross_dn, own, from_cross_up, from_axial_up)
    blank = jnp.zeros((blocks, width), jnp.float32)
    for place, source in zip(PLACES, sources):
        base = place * blocks * SUB
        for comp in range(3):
            x = source[comp]
            if place == 3:
                x = x * has_dn
            if place == 5:
                x = x * has_up
            high, low = high_low(x)
            ext[pl.ds(base + comp, blocks, stride=SUB), :] = high
            ext[pl.ds(base + LOW + comp, blocks, stride=SUB), :] = low
        ext[pl.ds(base + 3, blocks, stride=SUB), :] = blank
        ext[pl.ds(base + LOW + 3, blocks, stride=SUB), :] = blank
    acc[...] = jnp.zeros_like(acc)
    rows = lax.broadcasted_iota(jnp.int32, (SUB, width), 0)
    squares = jnp.zeros((SUB, width), jnp.float32)
    for b in range(blocks):
        starts = [pl.multiple_of(ids[b, k] * SUB, SUB) for k in range(count)]
        coupled = jnp.zeros((SUB, width), jnp.float32)
        for k in range(0, count, 2):
            picked = jnp.concatenate(
                [ext[pl.ds(starts[k], SUB), :], ext[pl.ds(starts[k + 1], SUB), :]], axis=1
            ).astype(jnp.bfloat16)
            pair = jnp.concatenate([tiles[b, k], tiles[b, k + 1]], axis=1)
            coupled += lax.dot_general(
                picked, pair, (((1,), (1,)), ((), ())), preferred_element_type=jnp.float32
            )
        coupled = coupled + pltpu.roll(coupled, LOW, 0)
        squares += jnp.where(rows < LOW, coupled * coupled, 0.0)
        high, low = high_low(coupled)
        parts = jnp.where(rows < LOW, high, low).astype(jnp.bfloat16)
        for k in range(count):
            acc[pl.ds(starts[k], SUB), :] += jnp.dot(
                parts, tiles[b, k], preferred_element_type=jnp.float32
            )
    targets = (to_axial_dn, to_cross_dn, None, to_cross_up, to_axial_up)
    even = jnp.zeros((blocks, width), jnp.float32)
    odd = squares
    for place, target in zip(PLACES, targets):
        base = place * blocks * SUB
        for comp in range(3):
            total = (
                acc[pl.ds(base + comp, blocks, stride=SUB), :]
                + acc[pl.ds(base + LOW + comp, blocks, stride=SUB), :]
            )
            if target is None:
                x = own[comp]
                dragged = drag[...] * x
                even += x * x
                odd += dragged * x
                kept[comp] = dragged + total
            else:
                target[comp] = total
    even = jnp.sum(even, axis=0, keepdims=True)
    odd = jnp.sum(odd, axis=0, keepdims=True)
    merged = jnp.where(
        rows == 2 * sweep, even, jnp.where(rows == 2 * sweep + 1, odd, carried[0][...])
    )
    moments[...] = jnp.broadcast_to(merged, moments.shape)
    if sweep == ITERS - 1:
        to_cross_dn[3] = carried[1][...]
        to_cross_up[3] = carried[1][...]


def operator_call(sweep, ids, sources, tiles, drag, carried, copies):
    blocks, width = drag.shape
    vmem = pl.BlockSpec(memory_space=pltpu.VMEM)
    field = jax.ShapeDtypeStruct((3, blocks, width), jnp.float32)
    across = jax.ShapeDtypeStruct((4 if sweep == ITERS - 1 else 3, blocks, width), jnp.float32)
    plane = (SUB, width) if copies is None else (copies, SUB, width)
    plane = jax.ShapeDtypeStruct(plane, jnp.float32)
    rows = (8 * blocks + 1) * SUB
    scratch = [pltpu.VMEM((rows, width), jnp.float32), pltpu.VMEM((rows, width), jnp.float32)]
    return pl.pallas_call(
        functools.partial(operator_kernel, sweep),
        in_specs=[pl.BlockSpec(memory_space=pltpu.SMEM)]
        + [vmem] * 5
        + [vmem] * (2 + len(carried)),
        out_specs=[vmem] * 6,
        out_shape=[field, across, across, field, field, plane],
        scratch_shapes=scratch,
        compiler_params=pltpu.CompilerParams(vmem_limit_bytes=4 << 20),
    )(ids, *sources, tiles, drag, *carried)


def shifted_poly(poly):
    return [None] + list(poly)


def combine(left, scale, right):
    out = []
    for i in range(max(len(left), len(right))):
        a = left[i] if i < len(left) else None
        b = right[i] if i < len(right) else None
        b = None if b is None else scale * b
        out.append(b if a is None else a if b is None else a + b)
    return out


def inner(left, right, shift, moment):
    total = None
    for i, a in enumerate(left):
        for j, b in enumerate(right):
            term = a * b * moment[i + j + shift]
            total = term if total is None else total + term
    return total


def cg_coefficients(moment):
    one = jnp.ones_like(moment[0])
    velocity, residual, direction = [], [one], [one]
    norm_now = moment[0]
    for sweep in range(ITERS):
        alpha = norm_now / inner(direction, direction, 1, moment)
        velocity = combine(velocity, alpha, direction)
        residual = combine(residual, -alpha, shifted_poly(direction))
        if sweep < ITERS - 1:
            norm_next = inner(residual, residual, 0, moment)
            direction = combine(residual, norm_next / norm_now, direction)
            norm_now = norm_next
    return velocity, residual


def mixed(coefs, fields):
    total = coefs[0] * fields[0]
    for c, f in zip(coefs[1:], fields[1:]):
        total = total + c * f
    return total


def picked_beads(fields, coefs, wanted, live):
    blocks, width = fields[0][0].shape
    index = jnp.where(live, wanted.astype(jnp.int32), -1)
    block = lax.shift_right_arithmetic(index, 7)
    place = jnp.bitwise_and(index, width - 1)
    parts = []
    for comp in range(3):
        x = mixed(coefs, [f[comp] for f in fields])
        high, rest = high_low(x)
        middle, low = high_low(rest)
        parts += [high, middle, low]
    stacked = jnp.concatenate(parts + [jnp.zeros_like(parts[0])], axis=0).astype(jnp.bfloat16)
    lanes = lax.broadcasted_iota(jnp.int32, (width, width), 0)
    chosen = jnp.where(lanes == place, 1.0, 0.0).astype(jnp.bfloat16)
    found = jnp.dot(stacked, chosen, preferred_element_type=jnp.float32)
    keep = lax.broadcasted_iota(jnp.int32, (blocks, width), 0) == block
    out = []
    for comp in range(3):
        at = 3 * comp * blocks
        x = (
            found[at : at + blocks]
            + found[at + blocks : at + 2 * blocks]
            + found[at + 2 * blocks : at + 3 * blocks]
        )
        out.append(jnp.sum(jnp.where(keep, x, 0.0), axis=0, keepdims=True))
    return out


def finish_kernel(
    sums, k0, k1, k2, k3, d0, d1, d2, u0, u1, u2, dn_plane, up_plane, velocity, residual, arrivals
):
    blocks, width = k0.shape[1:]
    slab = lax.axis_index("cross")
    total = jnp.sum(sums[...], axis=0)
    moment = [
        jnp.broadcast_to(jnp.sum(total[i : i + 1], axis=1, keepdims=True), (blocks, width))
        for i in range(2 * ITERS)
    ]
    vel, res = cg_coefficients(moment)
    own = (k0, k1, k2, k3)
    for comp in range(3):
        velocity[comp] = mixed(vel, [k[comp] for k in own[:ITERS]])
        residual[comp] = mixed(res, [k[comp] for k in own])
    lower = picked_beads((d0, d1, d2), vel, dn_plane[3, 1:2, :], slab > 0)
    upper = picked_beads(
        (u0, u1, u2), vel, up_plane[3, 0:1, :], slab < lax.axis_size("cross") - 1
    )
    for comp in range(3):
        arrivals[comp] = lower[comp] + upper[comp]


def finish_call(sums, own, below, above, planes):
    blocks, width = own[1].shape[1:]
    vmem = pl.BlockSpec(memory_space=pltpu.VMEM)
    field = jax.ShapeDtypeStruct((3, blocks, width), jnp.float32)
    return pl.pallas_call(
        finish_kernel,
        in_specs=[vmem] * 13,
        out_specs=[vmem] * 3,
        out_shape=[field, field, jax.ShapeDtypeStruct((3, 1, width), jnp.float32)],
        compiler_params=pltpu.CompilerParams(vmem_limit_bytes=4 << 20),
    )(sums, *own, *below, *above, *planes)


def no_moments_kernel(moments):
    moments[...] = jnp.zeros_like(moments)


def no_moments(width):
    return pl.pallas_call(
        no_moments_kernel,
        out_specs=pl.BlockSpec(memory_space=pltpu.VMEM),
        out_shape=jax.ShapeDtypeStruct((SUB, width), jnp.float32),
        compiler_params=pltpu.CompilerParams(vmem_limit_bytes=4 << 20),
        cost_estimate=pl.CostEstimate(
            flops=FIRST_EXCHANGE_FLOPS, bytes_accessed=4 * SUB * width, transcendentals=0
        ),
    )()


def leaving_rows(mig_rows, mig_count, blocks, width):
    capacity = mig_rows.shape[-1]
    live = lax.broadcasted_iota(jnp.int32, (2, capacity), 1) < mig_count[0, 0][:, None]
    rows = jnp.where(live, mig_rows[0, 0], -1).astype(jnp.float32)
    none = jnp.full((1, width - capacity), -1.0, jnp.float32)
    to_lower = jnp.concatenate([none, rows[0:1]], axis=1)
    to_upper = jnp.concatenate([rows[1:2], none], axis=1)
    rest = jnp.zeros((blocks - 2, width), jnp.float32)
    return jnp.concatenate([to_lower, to_upper, rest], axis=0)


def spread_sum(part, key):
    axial, cross = lax.axis_size("axial"), lax.axis_size("cross")
    groups = {}
    for a in range(axial):
        for c in range(cross):
            groups.setdefault(key(a, c), []).append(a * cross + c)
    groups = list(groups.values())
    if part.ndim == 2:
        part = jnp.broadcast_to(part[None], (len(groups[0]),) + part.shape)
    return lax.all_to_all(part, ("axial", "cross"), 0, 0, axis_index_groups=groups)


def on_device(force, self_drag, tiles, tile_ids, mig_rows, mig_count):
    field = jnp.swapaxes(force[0, 0], 0, 1)
    drag = self_drag[0, 0]
    blocks, width = drag.shape
    ids = tile_ids[0, 0]
    slab = lax.axis_index("cross")
    last = lax.axis_size("cross") - 1
    now, carried = field, (no_moments(width),)
    own, below, above, planes = [], [], [], []
    for sweep in range(ITERS):
        cross_dn = ring_shift(now, "cross", 1)
        cross_up = ring_shift(now, "cross", -1)
        axial_dn = ring_shift(now, "axial", 1)
        axial_up = ring_shift(now, "axial", -1)
        own.append(now)
        below.append(cross_dn)
        above.append(cross_up)
        r1, r3, r5, r7, kept, sums = operator_call(
            sweep, ids, (now, cross_up, axial_up, cross_dn, axial_dn), tiles[0, 0], drag, carried,
            2 * lax.axis_size("axial") if sweep == ITERS - 1 else None,
        )
        carried = (sums,)
        if sweep == ITERS - 1:
            part = jnp.sum(spread_sum(sums, lambda a, c: c // 2), axis=0)
            part, r1, r7 = lax.optimization_barrier((part, r1, r7))
        from_lower_cross = ring_shift(r5, "cross", 1)
        from_upper_cross = ring_shift(r3, "cross", -1)
        if sweep == ITERS - 1:
            part, from_lower_cross, from_upper_cross = lax.optimization_barrier(
                (part, from_lower_cross, from_upper_cross)
            )
            sums = spread_sum(part, lambda a, c: (a, c % 2))
        from_lower_axial = ring_shift(r7, "axial", 1)
        from_upper_axial = ring_shift(r1, "axial", -1)
        if sweep == ITERS - 1:
            planes = [from_lower_cross, from_upper_cross]
        now = kept + from_lower_axial
        now = now + jnp.where(slab > 0, from_lower_cross[:3], 0.0)
        now = now + from_upper_axial
        now = now + jnp.where(slab < last, from_upper_cross[:3], 0.0)
        if sweep == ITERS - 2:
            now, mig_rows, mig_count = lax.optimization_barrier((now, mig_rows, mig_count))
            carried += (leaving_rows(mig_rows, mig_count, blocks, width),)
    own.append(now)
    velocity, residual, arrivals = finish_call(sums, own, below, above, planes)
    return (
        jnp.swapaxes(velocity, 0, 1)[None, None],
        jnp.swapaxes(residual, 0, 1)[None, None],
        jnp.swapaxes(arrivals, 0, 1)[None],
    )


def solution(mesh):
    placed = (
        P("axial", "cross", None, None, None),
        P("axial", "cross", None, None),
        P("axial", "cross", None, None, None, None),
        P("axial", "cross", None, None),
        P("axial", "cross", None, None),
        P("axial", "cross", None),
    )
    return jax.shard_map(
        on_device,
        mesh=mesh,
        in_specs=placed,
        out_specs=(
            P("axial", "cross", None, None, None),
            P("axial", "cross", None, None, None),
            P("axial", "cross", None, None),
        ),
        check_vma=False,
    )
```

```python
import functools

import jax
import jax.numpy as jnp
from jax import lax
from jax.experimental import pallas as pl
from jax.experimental.pallas import tpu as pltpu
from jax.sharding import PartitionSpec as P

ITERS = 3
PLACES = (1, 3, 4, 5, 7)
SUB = 8
FIRST_EXCHANGE_FLOPS = 8 * 10**9
LOW = 4


def ring(count, by):
    return [(i, (i + by) % count) for i in range(count)]


def ring_shift(shard, axis, by):
    return lax.ppermute(shard, axis, ring(lax.axis_size(axis), by))


def high_low(x):
    high = x.astype(jnp.bfloat16).astype(jnp.float32)
    return high, x - high


def operator_kernel(
    sweep, ids, own, from_cross_up, from_axial_up, from_cross_dn, from_axial_dn, tiles, drag, *rest
):
    many = 2 if sweep == ITERS - 1 else 1
    carried, rest = rest[:many], rest[many:]
    (
        to_axial_dn, to_cross_dn, to_cross_up, to_axial_up, kept, moments, ext, acc,
    ) = rest
    blocks, count = ids.shape
    width = tiles.shape[-1]
    slab = lax.axis_index("cross")
    has_dn = jnp.where(slab > 0, 1.0, 0.0).astype(jnp.float32)
    has_up = jnp.where(slab < lax.axis_size("cross") - 1, 1.0, 0.0).astype(jnp.float32)
    sources = (from_axial_dn, from_cross_dn, own, from_cross_up, from_axial_up)
    blank = jnp.zeros((blocks, width), jnp.float32)
    for place, source in zip(PLACES, sources):
        base = place * blocks * SUB
        for comp in range(3):
            x = source[comp]
            if place == 3:
                x = x * has_dn
            if place == 5:
                x = x * has_up
            high, low = high_low(x)
            ext[pl.ds(base + comp, blocks, stride=SUB), :] = high
            ext[pl.ds(base + LOW + comp, blocks, stride=SUB), :] = low
        ext[pl.ds(base + 3, blocks, stride=SUB), :] = blank
        ext[pl.ds(base + LOW + 3, blocks, stride=SUB), :] = blank
    acc[...] = jnp.zeros_like(acc)
    rows = lax.broadcasted_iota(jnp.int32, (SUB, width), 0)
    squares = jnp.zeros((SUB, width), jnp.float32)
    for b in range(blocks):
        starts = [pl.multiple_of(ids[b, k] * SUB, SUB) for k in range(count)]
        coupled = jnp.zeros((SUB, width), jnp.float32)
        for k in range(0, count, 2):
            picked = jnp.concatenate(
                [ext[pl.ds(starts[k], SUB), :], ext[pl.ds(starts[k + 1], SUB), :]], axis=1
            ).astype(jnp.bfloat16)
            pair = jnp.concatenate([tiles[b, k], tiles[b, k + 1]], axis=1)
            coupled += lax.dot_general(
                picked, pair, (((1,), (1,)), ((), ())), preferred_element_type=jnp.float32
            )
        coupled = coupled + pltpu.roll(coupled, LOW, 0)
        squares += jnp.where(rows < LOW, coupled * coupled, 0.0)
        high, low = high_low(coupled)
        parts = jnp.where(rows < LOW, high, low).astype(jnp.bfloat16)
        for k in range(count):
            acc[pl.ds(starts[k], SUB), :] += jnp.dot(
                parts, tiles[b, k], preferred_element_type=jnp.float32
            )
    targets = (to_axial_dn, to_cross_dn, None, to_cross_up, to_axial_up)
    even = jnp.zeros((blocks, width), jnp.float32)
    odd = squares
    for place, target in zip(PLACES, targets):
        base = place * blocks * SUB
        for comp in range(3):
            total = (
                acc[pl.ds(base + comp, blocks, stride=SUB), :]
                + acc[pl.ds(base + LOW + comp, blocks, stride=SUB), :]
            )
            if target is None:
                x = own[comp]
                dragged = drag[...] * x
                even += x * x
                odd += dragged * x
                kept[comp] = dragged + total
            else:
                target[comp] = total
    even = jnp.sum(even, axis=0, keepdims=True)
    odd = jnp.sum(odd, axis=0, keepdims=True)
    merged = jnp.where(
        rows == 2 * sweep, even, jnp.where(rows == 2 * sweep + 1, odd, carried[0][...])
    )
    moments[...] = jnp.broadcast_to(merged, moments.shape)
    if sweep == ITERS - 1:
        to_cross_dn[3] = carried[1][...]
        to_cross_up[3] = carried[1][...]


def operator_call(sweep, ids, sources, tiles, drag, carried, copies):
    blocks, width = drag.shape
    vmem = pl.BlockSpec(memory_space=pltpu.VMEM)
    field = jax.ShapeDtypeStruct((3, blocks, width), jnp.float32)
    across = jax.ShapeDtypeStruct((4 if sweep == ITERS - 1 else 3, blocks, width), jnp.float32)
    plane = (SUB, width) if copies is None else (copies, SUB, width)
    plane = jax.ShapeDtypeStruct(plane, jnp.float32)
    rows = (8 * blocks + 1) * SUB
    scratch = [pltpu.VMEM((rows, width), jnp.float32), pltpu.VMEM((rows, width), jnp.float32)]
    return pl.pallas_call(
        functools.partial(operator_kernel, sweep),
        in_specs=[pl.BlockSpec(memory_space=pltpu.SMEM)]
        + [vmem] * 5
        + [vmem] * (2 + len(carried)),
        out_specs=[vmem] * 6,
        out_shape=[field, across, across, field, field, plane],
        scratch_shapes=scratch,
        compiler_params=pltpu.CompilerParams(vmem_limit_bytes=4 << 20),
    )(ids, *sources, tiles, drag, *carried)


def shifted_poly(poly):
    return [None] + list(poly)


def combine(left, scale, right):
    out = []
    for i in range(max(len(left), len(right))):
        a = left[i] if i < len(left) else None
        b = right[i] if i < len(right) else None
        b = None if b is None else scale * b
        out.append(b if a is None else a if b is None else a + b)
    return out


def inner(left, right, shift, moment):
    total = None
    for i, a in enumerate(left):
        for j, b in enumerate(right):
            term = a * b * moment[i + j + shift]
            total = term if total is None else total + term
    return total


def cg_coefficients(moment):
    one = jnp.ones_like(moment[0])
    velocity, residual, direction = [], [one], [one]
    norm_now = moment[0]
    for sweep in range(ITERS):
        alpha = norm_now / inner(direction, direction, 1, moment)
        velocity = combine(velocity, alpha, direction)
        residual = combine(residual, -alpha, shifted_poly(direction))
        if sweep < ITERS - 1:
            norm_next = inner(residual, residual, 0, moment)
            direction = combine(residual, norm_next / norm_now, direction)
            norm_now = norm_next
    return velocity, residual


def mixed(coefs, fields):
    total = coefs[0] * fields[0]
    for c, f in zip(coefs[1:], fields[1:]):
        total = total + c * f
    return total


def picked_beads(fields, coefs, wanted, live):
    blocks, width = fields[0][0].shape
    index = jnp.where(live, wanted.astype(jnp.int32), -1)
    block = lax.shift_right_arithmetic(index, 7)
    place = jnp.bitwise_and(index, width - 1)
    parts = []
    for comp in range(3):
        x = mixed(coefs, [f[comp] for f in fields])
        high, rest = high_low(x)
        middle, low = high_low(rest)
        parts += [high, middle, low]
    stacked = jnp.concatenate(parts + [jnp.zeros_like(parts[0])], axis=0).astype(jnp.bfloat16)
    lanes = lax.broadcasted_iota(jnp.int32, (width, width), 0)
    chosen = jnp.where(lanes == place, 1.0, 0.0).astype(jnp.bfloat16)
    found = jnp.dot(stacked, chosen, preferred_element_type=jnp.float32)
    keep = lax.broadcasted_iota(jnp.int32, (blocks, width), 0) == block
    out = []
    for comp in range(3):
        at = 3 * comp * blocks
        x = (
            found[at : at + blocks]
            + found[at + blocks : at + 2 * blocks]
            + found[at + 2 * blocks : at + 3 * blocks]
        )
        out.append(jnp.sum(jnp.where(keep, x, 0.0), axis=0, keepdims=True))
    return out


def finish_kernel(
    sums, k0, k1, k2, k3, d0, d1, d2, u0, u1, u2, dn_plane, up_plane, velocity, residual, arrivals
):
    blocks, width = k0.shape[1:]
    slab = lax.axis_index("cross")
    total = jnp.sum(sums[...], axis=0)
    moment = [
        jnp.broadcast_to(jnp.sum(total[i : i + 1], axis=1, keepdims=True), (blocks, width))
        for i in range(2 * ITERS)
    ]
    vel, res = cg_coefficients(moment)
    own = (k0, k1, k2, k3)
    for comp in range(3):
        velocity[comp] = mixed(vel, [k[comp] for k in own[:ITERS]])
        residual[comp] = mixed(res, [k[comp] for k in own])
    lower = picked_beads((d0, d1, d2), vel, dn_plane[3, 1:2, :], slab > 0)
    upper = picked_beads(
        (u0, u1, u2), vel, up_plane[3, 0:1, :], slab < lax.axis_size("cross") - 1
    )
    for comp in range(3):
        arrivals[comp] = lower[comp] + upper[comp]


def finish_call(sums, own, below, above, planes):
    blocks, width = own[1].shape[1:]
    vmem = pl.BlockSpec(memory_space=pltpu.VMEM)
    field = jax.ShapeDtypeStruct((3, blocks, width), jnp.float32)
    return pl.pallas_call(
        finish_kernel,
        in_specs=[vmem] * 13,
        out_specs=[vmem] * 3,
        out_shape=[field, field, jax.ShapeDtypeStruct((3, 1, width), jnp.float32)],
        compiler_params=pltpu.CompilerParams(vmem_limit_bytes=4 << 20),
    )(sums, *own, *below, *above, *planes)


def no_moments_kernel(moments):
    moments[...] = jnp.zeros_like(moments)


def no_moments(width):
    return pl.pallas_call(
        no_moments_kernel,
        out_specs=pl.BlockSpec(memory_space=pltpu.VMEM),
        out_shape=jax.ShapeDtypeStruct((SUB, width), jnp.float32),
        compiler_params=pltpu.CompilerParams(vmem_limit_bytes=4 << 20),
        cost_estimate=pl.CostEstimate(
            flops=FIRST_EXCHANGE_FLOPS, bytes_accessed=4 * SUB * width, transcendentals=0
        ),
    )()


def leaving_rows(mig_rows, mig_count, blocks, width):
    capacity = mig_rows.shape[-1]
    live = lax.broadcasted_iota(jnp.int32, (2, capacity), 1) < mig_count[0, 0][:, None]
    rows = jnp.where(live, mig_rows[0, 0], -1).astype(jnp.float32)
    none = jnp.full((1, width - capacity), -1.0, jnp.float32)
    to_lower = jnp.concatenate([none, rows[0:1]], axis=1)
    to_upper = jnp.concatenate([rows[1:2], none], axis=1)
    rest = jnp.zeros((blocks - 2, width), jnp.float32)
    return jnp.concatenate([to_lower, to_upper, rest], axis=0)


def spread_sum(part, key):
    axial, cross = lax.axis_size("axial"), lax.axis_size("cross")
    groups = {}
    for a in range(axial):
        for c in range(cross):
            groups.setdefault(key(a, c), []).append(a * cross + c)
    groups = list(groups.values())
    if part.ndim == 2:
        part = jnp.broadcast_to(part[None], (len(groups[0]),) + part.shape)
    return lax.all_to_all(part, ("axial", "cross"), 0, 0, axis_index_groups=groups)


def on_device(force, self_drag, tiles, tile_ids, mig_rows, mig_count):
    field = jnp.swapaxes(force[0, 0], 0, 1)
    drag = self_drag[0, 0]
    blocks, width = drag.shape
    ids = tile_ids[0, 0]
    slab = lax.axis_index("cross")
    last = lax.axis_size("cross") - 1
    now, carried = field, (no_moments(width),)
    own, below, above, planes = [], [], [], []
    for sweep in range(ITERS):
        cross_dn = ring_shift(now, "cross", 1)
        cross_up = ring_shift(now, "cross", -1)
        axial_dn = ring_shift(now, "axial", 1)
        axial_up = ring_shift(now, "axial", -1)
        own.append(now)
        below.append(cross_dn)
        above.append(cross_up)
        r1, r3, r5, r7, kept, sums = operator_call(
            sweep, ids, (now, cross_up, axial_up, cross_dn, axial_dn), tiles[0, 0], drag, carried,
            2 * lax.axis_size("axial") if sweep == ITERS - 1 else None,
        )
        carried = (sums,)
        if sweep == ITERS - 1:
            part = jnp.sum(spread_sum(sums, lambda a, c: c // 2), axis=0)
            part, r3, r5 = lax.optimization_barrier((part, r3, r5))
        from_lower_axial = ring_shift(r7, "axial", 1)
        from_upper_axial = ring_shift(r1, "axial", -1)
        if sweep == ITERS - 1:
            part, from_lower_axial, from_upper_axial = lax.optimization_barrier(
                (part, from_lower_axial, from_upper_axial)
            )
            sums = spread_sum(part, lambda a, c: (a, c % 2))
        from_lower_cross = ring_shift(r5, "cross", 1)
        from_upper_cross = ring_shift(r3, "cross", -1)
        if sweep == ITERS - 1:
            planes = [from_lower_cross, from_upper_cross]
        now = kept + from_lower_axial
        now = now + jnp.where(slab > 0, from_lower_cross[:3], 0.0)
        now = now + from_upper_axial
        now = now + jnp.where(slab < last, from_upper_cross[:3], 0.0)
        if sweep == ITERS - 2:
            now, mig_rows, mig_count = lax.optimization_barrier((now, mig_rows, mig_count))
            carried += (leaving_rows(mig_rows, mig_count, blocks, width),)
    own.append(now)
    velocity, residual, arrivals = finish_call(sums, own, below, above, planes)
    return (
        jnp.swapaxes(velocity, 0, 1)[None, None],
        jnp.swapaxes(residual, 0, 1)[None, None],
        jnp.swapaxes(arrivals, 0, 1)[None],
    )


def solution(mesh):
    placed = (
        P("axial", "cross", None, None, None),
        P("axial", "cross", None, None),
        P("axial", "cross", None, None, None, None),
        P("axial", "cross", None, None),
        P("axial", "cross", None, None),
        P("axial", "cross", None),
    )
    return jax.shard_map(
        on_device,
        mesh=mesh,
        in_specs=placed,
        out_specs=(
            P("axial", "cross", None, None, None),
            P("axial", "cross", None, None, None),
            P("axial", "cross", None, None),
        ),
        check_vma=False,
    )
```
